32 devices in a mesh: grp: 2 (over y), hold: 4 (over z), tp: 2 (over x), rep: 2 (over core).
Axes of the slice: x: 2, y: 2, z: 4, core: 2. Of those that a mesh axis runs over, the one named last changes fastest.
Arguments:
- cache: bfloat16 [8, 4, 8, 5120], P(('grp', 'hold'), None, ('tp', 'rep')), parts along dimension 0, may hold values from -6 to 6
- ln_gain: float32 [1280], replicated, may hold values from 0.5 to 1.5
- w_fc1: bfloat16 [5120, 2560], P('hold', ('tp', 'rep')), may hold values from -0.078125 to 0.078125
- w_fc2: bfloat16 [2560, 4096], P('hold', ('tp', 'rep'))
- norm_gain: float32 [4096], P(('tp', 'rep')), may hold values from 0.5 to 1.5
- w_key: bfloat16 [4096, 1024], P(('tp', 'rep'), 'hold'), may hold values from -0.09375 to 0.09375
- matching: int32 [8, 4], P('grp'), parts along dimension 0, may hold values from 0 to 3, as said below
- counts: int32 [8, 4, 4], P(('grp', 'hold'), None, ('tp', 'rep')), parts along dimension 0, may hold values from 1 to 2
Outputs:
- keys: bfloat16 [8, 4, 8, 1024], P(('grp', 'hold'), None, ('tp', 'rep')), parts along dimension 0
The draws below stay inside these ranges and needn't reach their ends.
There are 2 independent parts, one for each index of `grp`. The reference program is written for one: setup_inputs(seed, part) draws one part's arguments, and reference() takes and returns one part's arrays. A program takes and returns all parts, laid end to end along the dimension named above; an argument that names none is the same for every part. Nothing has to cross between parts.
Inputs may be any that keep to these rules, and one draw needn't show every extreme that they name: Every row and every column of matching holds each owner once (each round is a perfect matching of holders to owners, and over the rounds each holder meets each owner once).
All inputs are finite; a program needn't handle non-finite values.
Results may differ from the reference program's by a relative error of at most 0.0068.
Values may be sent and summed in bfloat16 or wider, within the bound.
No kernel may reach another device: no remote copies, remote signals or barrier semaphores. Data moves between devices by JAX's collectives and lax.ppermute only.
A program may use at most 64 MiB of HBM per device.

```python
import jax
import jax.numpy as jnp
from jax import lax

VD = 1280
HM = 2560
DM = 4096
KD = 1024
BLK = 2
HOLDERS = 4
GROUP = 4


def draw_matching(key, part):
    key = jax.random.fold_in(key, 11)
    first, second, third = jax.random.split(key, 3)
    labels = jax.random.permutation(first, HOLDERS)
    row_shift = jax.random.permutation(second, HOLDERS)
    col_shift = jax.random.permutation(third, HOLDERS)
    return labels[(row_shift[:, None] + col_shift[None, :]) % HOLDERS].astype(jnp.int32)


def draw_w_fc2(key, part):
    key = jax.random.fold_in(key, 23)
    first, second = jax.random.split(key, 2)
    position = jnp.arange(DM, dtype=jnp.float32) / DM
    rough = jnp.exp(jax.random.uniform(second, (DM,), jnp.float32, -0.35, 0.35))
    values = jax.random.normal(first, (HM, DM), jnp.float32)
    ramp = 10.0 ** position
    return (values * (ramp * rough)[None, :] * HM ** (-0.5)).astype(jnp.bfloat16)


def set_ends(drawn, stream_key, low, largest):
    dims = drawn.shape
    place = [jax.random.randint(jax.random.fold_in(stream_key, axis), (), 0, dims[axis]) for axis in range(len(dims))]
    drawn = drawn.at[tuple(place)].set(low)
    longest = dims.index(max(dims))
    place[longest] = (place[longest] + 1) % dims[longest]
    return drawn.at[tuple(place)].set(largest)


def block_scale(rng, shape, shards, low, high):
    def one(dim, shards_of):
        draws = jax.random.uniform(jax.random.fold_in(jax.random.fold_in(rng, 6), dim), (shards_of,), jnp.float32, low / len(shards), high / len(shards))
        return jnp.repeat(jnp.exp(draws), shape[dim] // shards_of).reshape((-1,) + (1,) * (len(shape) - dim - 1))

    level = one(*shards[0])
    for cut in shards[1:]:
        level = level * one(*cut)
    return level


def gaussian(stream_key, shape, scale, bound, cuts=(), kind=jnp.bfloat16):
    loudness = block_scale(stream_key, shape, cuts, -0.22, 0.18) if cuts else 1.0
    array = jax.random.normal(stream_key, shape, jnp.float32) * scale * loudness
    return jnp.minimum(jnp.maximum(array, -bound), bound).astype(kind)


def setup_inputs(seed: int = 0, part: int = 0) -> dict:
    arg_keys = jax.random.split(jax.random.key(seed), 9)
    own_keys = jax.random.split(jax.random.fold_in(arg_keys[8], part), 9)
    cache = gaussian(own_keys[0], (HOLDERS, HOLDERS, GROUP * BLK, 4 * VD), 1.0, 6.0, ((0, 4), (2, 4)))
    ln_gain = jnp.clip(jax.random.uniform(arg_keys[1], (VD,), jnp.float32, 0.5, 1.5), 0.5, 1.5)
    w_fc1 = gaussian(arg_keys[2], (4 * VD, HM), (4 * VD) ** -0.5, 0.078125, ((0, 4), (1, 4)))
    w_fc2 = draw_w_fc2(jax.random.fold_in(arg_keys[8], 71), part)
    norm_gain = jnp.clip(0.5 + 1.0 * jax.random.uniform(arg_keys[4], (DM,), jnp.float32) ** block_scale(arg_keys[4], (DM,), ((0, 4),), -0.2, 0.2), 0.5, 1.5)
    w_key = gaussian(arg_keys[5], (DM, KD), DM ** -0.5, 0.09375, ((0, 4), (1, 4)))
    matching = draw_matching(jax.random.fold_in(jax.random.fold_in(arg_keys[8], part), 71), part)
    counts = set_ends(jax.random.randint(own_keys[7], (HOLDERS, HOLDERS, GROUP), 1, BLK + 1), jax.random.fold_in(own_keys[7], 1), 1, BLK).astype(jnp.int32)
    return {"cache": cache, "ln_gain": ln_gain, "w_fc1": w_fc1, "w_fc2": w_fc2, "norm_gain": norm_gain, "w_key": w_key, "matching": matching, "counts": counts}


EPSILON = 1e-06

def patch_norm(rows, ln_gain):
    width = ln_gain.shape[0]
    patches = rows.astype(jnp.float32).reshape(rows.shape[0], -1, width)
    scale = lax.rsqrt(lax.optimization_barrier(jnp.mean(patches * patches, axis=2, keepdims=True)) + EPSILON)
    return (patches * scale * ln_gain).reshape(rows.shape[0], -1).astype(jnp.bfloat16)

def reference(cache, ln_gain, w_fc1, w_fc2, norm_gain, w_key, matching, counts):
    holders = matching.shape[0]
    owners = jnp.arange(holders, dtype=jnp.int32)
    sources = jnp.argmax(matching[None, :, :] == owners[:, None, None], axis=2).astype(jnp.int32)
    rounds = jnp.arange(holders, dtype=jnp.int32)[None, :]
    delivered = cache[sources, rounds]
    live = counts[sources, rounds]

    def one_owner(inputs):
        blocks, owner_counts = inputs
        normed = patch_norm(blocks.reshape(-1, blocks.shape[-1]), ln_gain)
        hidden = jax.nn.gelu(jnp.dot(normed, w_fc1, preferred_element_type=jnp.float32), approximate=False).astype(jnp.bfloat16)
        merged = jnp.dot(hidden, w_fc2, preferred_element_type=jnp.float32)
        scale = lax.rsqrt(lax.optimization_barrier(jnp.sum(merged * merged, axis=1)) / DM + EPSILON)
        features = (merged * scale[:, None] * norm_gain).astype(jnp.bfloat16)
        keys = jnp.dot(features, w_key, preferred_element_type=jnp.float32).reshape(holders, -1, BLK, KD)
        valid = jnp.arange(BLK, dtype=jnp.int32)[None, None, :] < owner_counts[:, :, None]
        keys = jnp.where(valid[..., None], keys, jnp.zeros_like(keys))
        return keys.reshape(holders, -1, KD).astype(jnp.bfloat16)
    return lax.map(one_owner, (delivered, live))
```

```python
import jax
import jax.numpy as jnp
from jax import lax
from jax.sharding import PartitionSpec as P

EPSILON = 1e-06
GROUP_AXES = ("tp", "rep")
ALL_AXES = ("hold", "tp", "rep")


def patch_norm(rows, ln_gain):
    width = ln_gain.shape[0]
    patches = rows.astype(jnp.float32).reshape(rows.shape[0], -1, width)
    scale = lax.rsqrt(jnp.mean(patches * patches, axis=2, keepdims=True) + EPSILON)
    return patches * scale * ln_gain


def merger_features(rows, ln_gain, w_fc1, w_fc2, norm_gain, width):
    normed = patch_norm(rows, ln_gain).reshape(rows.shape[0], -1).astype(jnp.bfloat16)
    first_cols = lax.all_gather(w_fc1, "hold", axis=0, tiled=True)
    product = jnp.dot(
        lax.all_gather(normed, GROUP_AXES, axis=0, tiled=True),
        first_cols,
        preferred_element_type=jnp.float32,
    )
    hidden = jax.nn.gelu(product, approximate=False).astype(jnp.bfloat16)
    second_cols = lax.all_gather(w_fc2, "hold", axis=0, tiled=True)
    merged = jnp.dot(
        lax.all_gather(hidden, GROUP_AXES, axis=1, tiled=True),
        second_cols,
        preferred_element_type=jnp.float32,
    )
    squares = lax.psum(jnp.sum(merged * merged, axis=1), GROUP_AXES)
    scale = lax.rsqrt(squares / width + EPSILON)
    return (merged * scale[:, None] * norm_gain).astype(jnp.bfloat16)


def rows_to_owners(cache, ln_gain, w_fc1, w_fc2, norm_gain, w_key, matching, counts, width):
    rounds = cache.shape[1]
    block = cache.shape[2]
    holder_index = lax.axis_index("hold")
    owner_column = lax.dynamic_slice_in_dim(matching, holder_index, 1, 1)[:, 0]
    send_order = jnp.argsort(owner_column)
    source_of = jnp.argmax(matching == holder_index, axis=1)
    sent_counts = jnp.take(counts[0, :, 0], send_order)
    outgoing = jnp.take(cache[0], send_order, axis=0)
    arrived = lax.all_to_all(outgoing, "hold", split_axis=0, concat_axis=0, tiled=True)
    arrived_counts = lax.all_to_all(
        sent_counts.reshape(rounds, 1), "hold", split_axis=0, concat_axis=0, tiled=True
    )
    own_blocks = jnp.take(arrived, source_of, axis=0)
    own_counts = jnp.take(arrived_counts[:, 0], source_of)
    features = merger_features(
        own_blocks.reshape(rounds * block, -1), ln_gain, w_fc1, w_fc2, norm_gain, width
    )
    key_cols = lax.all_gather(w_key, "hold", axis=1, tiled=True)
    keys = lax.psum_scatter(
        jnp.dot(features, key_cols, preferred_element_type=jnp.float32),
        GROUP_AXES,
        scatter_dimension=0,
        tiled=True,
    )
    keys = keys.reshape(rounds, block, -1)
    valid = jnp.arange(block, dtype=jnp.int32)[None, :] < own_counts[:, None]
    keys = jnp.where(valid[:, :, None], keys, jnp.zeros_like(keys))
    return keys.astype(jnp.bfloat16)[None]


def swap(x, axis, n, step):
    return lax.ppermute(x, axis, [(i, i ^ step) for i in range(n)])


def rows_past_weights(cache, ln_gain, w_fc1, w_fc2, norm_gain, w_key, matching, counts, width):
    n = lax.axis_size("hold")
    rounds, block, depth = cache.shape[1:]
    h = lax.axis_index("hold")
    t = lax.axis_index("tp") * lax.axis_size("rep") + lax.axis_index("rep")
    rows = rounds * block
    chunk = depth // n
    f32, bf16 = jnp.float32, jnp.bfloat16

    key_cols = lax.all_gather(w_key, "hold", axis=0, tiled=False)

    owner_column = lax.dynamic_slice_in_dim(matching, h, 1, 1)[:, 0]
    live = (jnp.arange(block)[None, :] < counts[0, :, 0][:, None]).astype(f32)
    place = (owner_column[None, :] == jnp.arange(n)[:, None]).astype(f32)
    pick = place[:, :, None] * live[None]
    normed = patch_norm(cache[0].reshape(rows, depth), ln_gain).astype(bf16).astype(f32)
    normed = normed.reshape(rounds, block, depth)
    by_owner = sum(pick[:, r, :, None] * normed[r][None] for r in range(rounds))
    by_chunk = by_owner.reshape(rows, n, chunk).transpose(1, 0, 2).astype(bf16)

    def chunk_of(s):
        return lax.dynamic_index_in_dim(by_chunk, h ^ s, 0, keepdims=False)

    mine = [chunk_of(0)] + [swap(chunk_of(s), "hold", n, s) for s in range(1, n)]
    group_rows = lax.all_gather(jnp.stack(mine), GROUP_AXES, axis=0, tiled=False)
    partial = jnp.dot(
        group_rows.reshape(n * n * rows, chunk), w_fc1, preferred_element_type=f32
    ).reshape(n, n, rows, -1)

    parts = []
    for k in range(n):
        perm = [(a * n + b, b * n + (a ^ k)) for a in range(n) for b in range(n)]
        parts.append(lax.ppermute(partial[:, k].astype(bf16), ALL_AXES, perm).astype(f32))
    product = sum(parts)
    hidden = jax.nn.gelu(product, approximate=False).astype(bf16)

    hidden = lax.all_gather(hidden, GROUP_AXES, axis=0, tiled=False)
    total = n * n * rows
    hidden = hidden.reshape(total, -1)
    to = jnp.arange(total)
    k_of, rest = to // (n * rows), to % (n * rows)
    slot_of, rest = rest // rows, rest % rows
    holder_of, b_of = rest // block, rest % block
    source = ((holder_of * n + slot_of) * n + (k_of ^ h)) * block + b_of
    order = (source[:, None] == jnp.arange(total)[None, :]).astype(bf16)
    hidden = jnp.dot(order, hidden, preferred_element_type=f32).astype(bf16)
    partial = jnp.dot(hidden, w_fc2, preferred_element_type=f32).reshape(n, n * rows, -1)
    merged = sum(
        [partial[0]]
        + [swap(partial[k].astype(bf16), "hold", n, k).astype(f32) for k in range(1, n)]
    )

    squares = jnp.sum(merged * merged, axis=1, keepdims=True)
    features = (merged * norm_gain).astype(bf16)
    keys = [jnp.dot(features, key_cols[i], preferred_element_type=f32) for i in range(n)]
    keys = jnp.concatenate(keys + [jnp.broadcast_to(squares, (n * rows, 128))], axis=1)
    keys = keys.reshape(n, rows, -1)

    def slot(u):
        return lax.dynamic_index_in_dim(keys, t ^ u, 0, keepdims=False)

    keys = slot(0) + sum(swap(slot(u), GROUP_AXES, n, u) for u in range(1, n))
    keys = keys[:, :-128] * lax.rsqrt(keys[:, -1:] / width + EPSILON)
    keys = keys.reshape(n, block, -1)
    source_of = (matching == h).astype(f32)
    keys = sum(source_of[:, i, None, None] * keys[i][None] for i in range(n))
    return keys.astype(bf16)[None]


def per_device(cache, ln_gain, w_fc1, w_fc2, norm_gain, w_key, matching, counts):
    hold = lax.axis_size("hold")
    group = lax.axis_size("tp") * lax.axis_size("rep")
    rounds, block, depth = cache.shape[1:]
    width = w_key.shape[0] * group
    few = hold * rounds * group * block <= w_fc1.shape[1]
    square = hold == group == rounds and hold & (hold - 1) == 0
    plan = rows_past_weights if few and square else rows_to_owners
    return plan(cache, ln_gain, w_fc1, w_fc2, norm_gain, w_key, matching, counts, width)


def solution(mesh):
    return jax.shard_map(
        per_device,
        mesh=mesh,
        in_specs=(
            P(("grp", "hold"), None, ("tp", "rep"), None),
            P(),
            P("hold", ("tp", "rep")),
            P("hold", ("tp", "rep")),
            P(("tp", "rep")),
            P(("tp", "rep"), "hold"),
            P("grp", None),
            P(("grp", "hold"), None, ("tp", "rep")),
        ),
        out_specs=P(("grp", "hold"), None, ("tp", "rep"), None),
        check_vma=False,
    )
```

```python
import functools

import jax
import jax.numpy as jnp
from jax import lax
from jax.experimental import pallas as pl
from jax.experimental.pallas import tpu as pltpu
from jax.sharding import PartitionSpec as P

EPSILON = 1e-06
GROUP_AXES = ("tp", "rep")
ALL_AXES = ("hold", "tp", "rep")


def patch_norm(rows, ln_gain):
    width = ln_gain.shape[0]
    patches = rows.astype(jnp.float32).reshape(rows.shape[0], -1, width)
    scale = lax.rsqrt(jnp.mean(patches * patches, axis=2, keepdims=True) + EPSILON)
    return patches * scale * ln_gain


def merger_features(rows, ln_gain, w_fc1, w_fc2, norm_gain, width):
    normed = patch_norm(rows, ln_gain).reshape(rows.shape[0], -1).astype(jnp.bfloat16)
    first_cols = lax.all_gather(w_fc1, "hold", axis=0, tiled=True)
    product = jnp.dot(
        lax.all_gather(normed, GROUP_AXES, axis=0, tiled=True),
        first_cols,
        preferred_element_type=jnp.float32,
    )
    hidden = jax.nn.gelu(product, approximate=False).astype(jnp.bfloat16)
    second_cols = lax.all_gather(w_fc2, "hold", axis=0, tiled=True)
    merged = jnp.dot(
        lax.all_gather(hidden, GROUP_AXES, axis=1, tiled=True),
        second_cols,
        preferred_element_type=jnp.float32,
    )
    squares = lax.psum(jnp.sum(merged * merged, axis=1), GROUP_AXES)
    scale = lax.rsqrt(squares / width + EPSILON)
    return (merged * scale[:, None] * norm_gain).astype(jnp.bfloat16)


def rows_to_owners(cache, ln_gain, w_fc1, w_fc2, norm_gain, w_key, matching, counts, width):
    rounds = cache.shape[1]
    block = cache.shape[2]
    holder_index = lax.axis_index("hold")
    owner_column = lax.dynamic_slice_in_dim(matching, holder_index, 1, 1)[:, 0]
    send_order = jnp.argsort(owner_column)
    source_of = jnp.argmax(matching == holder_index, axis=1)
    sent_counts = jnp.take(counts[0, :, 0], send_order)
    outgoing = jnp.take(cache[0], send_order, axis=0)
    arrived = lax.all_to_all(outgoing, "hold", split_axis=0, concat_axis=0, tiled=True)
    arrived_counts = lax.all_to_all(
        sent_counts.reshape(rounds, 1), "hold", split_axis=0, concat_axis=0, tiled=True
    )
    own_blocks = jnp.take(arrived, source_of, axis=0)
    own_counts = jnp.take(arrived_counts[:, 0], source_of)
    features = merger_features(
        own_blocks.reshape(rounds * block, -1), ln_gain, w_fc1, w_fc2, norm_gain, width
    )
    key_cols = lax.all_gather(w_key, "hold", axis=1, tiled=True)
    keys = lax.psum_scatter(
        jnp.dot(features, key_cols, preferred_element_type=jnp.float32),
        GROUP_AXES,
        scatter_dimension=0,
        tiled=True,
    )
    keys = keys.reshape(rounds, block, -1)
    valid = jnp.arange(block, dtype=jnp.int32)[None, :] < own_counts[:, None]
    keys = jnp.where(valid[:, :, None], keys, jnp.zeros_like(keys))
    return keys.astype(jnp.bfloat16)[None]


def swap(x, axis, n, step):
    return lax.ppermute(x, axis, [(i, i ^ step) for i in range(n)])


def call(body, outs, *args, flops=0, scratch=(), **specs):
    moved = sum(x.size * x.dtype.itemsize for x in args)
    return pl.pallas_call(
        body,
        out_shape=outs,
        scratch_shapes=scratch,
        cost_estimate=pl.CostEstimate(flops=flops, bytes_accessed=moved, transcendentals=0),
        compiler_params=pltpu.CompilerParams(vmem_limit_bytes=16 << 20),
        **specs,
    )(*args)


def dot(a, b):
    return jnp.dot(a, b, preferred_element_type=jnp.float32)


def norm_kernel(cache, ln_gain, matching, counts, w_fc1, w_key, *refs):
    outs, w_held, key_rows = refs[:4], refs[4], refs[5:9]
    x_in, gain_in, plan_in, live_in, held, sems = refs[9:]
    n = len(outs)
    h = lax.axis_index("hold")
    share = key_rows[0].shape[0]
    pairs = [(cache, x_in), (ln_gain, gain_in), (matching, plan_in), (counts, live_in)]
    for s in range(n):
        start = pl.multiple_of((h ^ s) * share, 128)
        pairs.append((w_key.at[pl.ds(start, share)], key_rows[s]))
    pairs.append((w_fc1, w_held))
    copies = [pltpu.make_async_copy(a, b, sems.at[i]) for i, (a, b) in enumerate(pairs)]
    for copy in copies:
        copy.start()
    for copy in copies[:4]:
        copy.wait()
    _, rounds, block, depth = cache.shape
    width = ln_gain.shape[0]
    chunk = depth // n
    gain = gain_in[...].reshape(1, width)
    column = lax.broadcasted_iota(jnp.int32, matching.shape, 1) == h
    owner = jnp.sum(jnp.where(column, plan_in[...], 0), axis=1, keepdims=True)
    b_of = lax.broadcasted_iota(jnp.int32, (block, 1), 0)
    for p in range(depth // width):
        cols = pl.ds(p * width, width)
        normed = []
        for r in range(rounds):
            x = x_in[0, r, :, cols].astype(jnp.float32)
            scale = lax.rsqrt(jnp.mean(x * x, axis=1, keepdims=True) + EPSILON)
            scale = jnp.where(b_of < live_in[:, r : r + 1], scale, 0.0)
            normed.append(x * scale * gain)
        for j in range(rounds):
            picked = sum(
                jnp.where(owner[r : r + 1] == j, normed[r], 0.0) for r in range(rounds)
            )
            held[j * block : (j + 1) * block, cols] = picked
    for s in range(n):
        start = pl.multiple_of((h ^ s) * chunk, 128)
        outs[s][...] = held[:, pl.ds(start, chunk)].astype(jnp.bfloat16)
    for copy in copies[4:]:
        copy.wait()


def first_kernel(mine, other, *refs):
    weights, outs = refs[:2], refs[2:6]
    rows, sums = refs[6:]
    h, rep = lax.axis_index("hold"), lax.axis_index("rep")
    half = mine.shape[0]
    size = half // 4
    for b, part in enumerate((mine, other)):
        part = part[...].astype(jnp.float32)
        for s in range(4):
            start = pl.multiple_of(b * half + (h ^ s) * size, 8)
            rows[pl.ds(start, size), :] = part[s * size : (s + 1) * size]
    x = rows[...].astype(jnp.bfloat16)
    for i, weight in enumerate(weights):
        sums[rep ^ i] = dot(x, weight[...])
    for k, out in enumerate(outs):
        start = pl.multiple_of(((h ^ k) & 1) * half, 16)
        out[...] = sums[(h ^ k) >> 1, pl.ds(start, half), :].astype(jnp.bfloat16)


def second_kernel(first, second, w_mine, w_other, *refs):
    outs, sums = refs[:4], refs[4]
    h = lax.axis_index("hold")
    half = first.shape[0]
    bb = half // 16
    to = lax.broadcasted_iota(jnp.int32, (2 * half, half), 0)
    source = lax.broadcasted_iota(jnp.int32, (2 * half, half), 1)
    u, owner = to // half, (to % half) // (4 * bb)
    holder, b_of = (to % (4 * bb)) // bb, to % bb
    wanted = (u ^ (h >> 1)) * half + (holder * 4 + owner) * bb + b_of
    moved = 0.0
    for p, part in enumerate((first, second)):
        order = jnp.where(source + p * half == wanted, 1.0, 0.0)
        moved += dot(order.astype(jnp.bfloat16), part[...])
    moved = moved.astype(jnp.bfloat16)
    cols = outs[0].shape[1] // 2
    for p, weight in enumerate((w_mine, w_other)):
        sums[p] = dot(moved, weight[...])
        for k in range(4):
            start = pl.multiple_of((h ^ k) * cols, 128)
            part = sums[p, :, pl.ds(start, cols)].astype(jnp.bfloat16)
            outs[k][:, p * cols : (p + 1) * cols] = part


def key_kernel(*refs):
    parts, blocks, gains = refs[:4], refs[4:6], refs[6:8]
    kept, sent, held = refs[8:]
    h = lax.axis_index("hold")
    merged = sum(part[...].astype(jnp.float32) for part in parts)
    squares = jnp.sum(merged * merged, axis=1, keepdims=True)
    cols = merged.shape[1] // 2
    start = pl.multiple_of(h * cols, 128)
    features = []
    for p in range(2):
        gain = gains[p][pl.ds(start, cols)].reshape(1, cols)
        features.append((merged[:, p * cols : (p + 1) * cols] * gain).astype(jnp.bfloat16))
    width = blocks[0].shape[1]
    for s in range(4):
        start = pl.multiple_of((h ^ s) * width, 128)
        held[:, pl.ds(start, width)] = sum(
            dot(features[p], blocks[p][s * cols : (s + 1) * cols, :]) for p in range(2)
        )
    half = kept.shape[0]
    keys = 4 * width
    kept[:, :keys] = held[:half, :]
    kept[:, keys:] = jnp.broadcast_to(squares[:half], (half, 128))
    sent[:, :keys] = held[half:, :].astype(jnp.bfloat16)
    high = squares[half:].astype(jnp.bfloat16).astype(jnp.float32)
    lane = lax.broadcasted_iota(jnp.int32, (half, 128), 1)
    pair = jnp.where(lane < 64, high, squares[half:] - high)
    sent[:, keys:] = pair.astype(jnp.bfloat16)


def group_kernel(kept, came, *refs):
    outs, held = refs[:4], refs[4]
    h = lax.axis_index("hold")
    keys = kept.shape[1] - 128
    held[:, :keys] = kept[:, :keys] + came[:, :keys].astype(jnp.float32)
    pair = came[:, keys:].astype(jnp.float32)
    squares = kept[:, keys:] + pair[:, :1] + pair[:, 127:]
    held[:, keys:] = squares
    rows = outs[0].shape[0]
    for k in range(4):
        outs[k][...] = held[pl.ds(pl.multiple_of((h ^ k) * rows, 8), rows), :]


def last_kernel(width, *refs):
    parts, matching, out = refs[:4], refs[4], refs[5]
    h = lax.axis_index("hold")
    total = sum(part[...] for part in parts)
    keys = total[:, :-128] * lax.rsqrt(total[:, -1:] / width + EPSILON)
    _, rounds, block, _ = out.shape
    for r in range(rounds):
        picked = sum(
            jnp.where(matching[r : r + 1, i : i + 1] == h, keys[i * block : (i + 1) * block], 0.0)
            for i in range(rounds)
        )
        out[0, r] = picked.astype(jnp.bfloat16)


def rows_past_weights(cache, ln_gain, w_fc1, w_fc2, norm_gain, w_key, matching, counts, width):
    n = lax.axis_size("hold")
    rounds, block, depth = cache.shape[1:]
    rows = rounds * block
    chunk = depth // n
    hidden_cols, out_cols, key_cols = w_fc1.shape[1], w_fc2.shape[1], w_key.shape[1]
    share = w_key.shape[0] // n
    f32, bf16 = jnp.float32, jnp.bfloat16
    vmem = pltpu.VMEM

    def like(dims, kind=bf16):
        return jax.ShapeDtypeStruct(dims, kind)

    w_fc1_other = swap(w_fc1, "rep", 2, 1)
    w_fc2_other = swap(w_fc2, "rep", 2, 1)
    gain_other = swap(norm_gain, "rep", 2, 1)
    counts = counts.reshape(1, rounds)
    cache_in, w_fc1_in, w_key_in, ln_in, matching_in, counts_in = (
        pltpu.with_memory_space_constraint(x, pltpu.HBM)
        for x in (cache, w_fc1, w_key, ln_gain, matching, counts)
    )
    *chunks, w_fc1_mine, key_0, key_1, key_2, key_3 = call(
        norm_kernel,
        [like((rows, chunk))] * n + [like(w_fc1.shape)] + [like((share, key_cols))] * n,
        cache_in,
        ln_in,
        matching_in,
        counts_in,
        w_fc1_in,
        w_key_in,
        in_specs=[pl.BlockSpec(memory_space=pltpu.HBM)] * 6,
        scratch=[
            vmem(cache.shape, bf16),
            vmem(ln_gain.shape, f32),
            vmem(matching.shape, jnp.int32),
            vmem(counts.shape, jnp.int32),
            vmem((rows, depth), f32),
            pltpu.SemaphoreType.DMA((9,)),
        ],
    )
    group_rows = jnp.concatenate(
        [swap(chunks[s], "hold", n, s) if s else chunks[s] for s in range(n)], axis=0
    )
    group_rows, w_fc1_other, w_fc2_other, gain_other, key_1, key_2, key_3 = (
        lax.optimization_barrier(
            (group_rows, w_fc1_other, w_fc2_other, gain_other, key_1, key_2, key_3)
        )
    )
    key_1, key_2, key_3 = (
        swap(part, "hold", n, s + 1) for s, part in enumerate((key_1, key_2, key_3))
    )

    partial = call(
        first_kernel,
        [like((4 * rows, hidden_cols))] * n,
        group_rows,
        swap(group_rows, "tp", 2, 1),
        w_fc1_mine,
        w_fc1_other,
        scratch=[vmem((8 * rows, chunk), f32), vmem((2, 8 * rows, hidden_cols), f32)],
        flops=32 * rows * w_fc1.size,
    )
    *partial, key_1 = lax.optimization_barrier((*partial, key_1))
    parts = [swap(partial[k], "hold", n, k) if k else partial[k] for k in range(n)]
    product = sum(part.astype(f32) for part in parts)
    hidden = jax.nn.gelu(product, approximate=False).astype(bf16)

    hidden, key_2, key_3 = lax.optimization_barrier((hidden, key_2, key_3))
    key_mine = jnp.concatenate([key_0, key_1, key_2, key_3])
    key_other = swap(key_mine, "rep", 2, 1)

    halves = []
    for g in range(2):
        perm = [
            (2 * a + b, 2 * (2 * b + (a >> 1)) + ((a & 1) ^ g)) for a in range(n) for b in range(2)
        ]
        halves.append(lax.ppermute(hidden, ("hold", "tp"), perm))

    merged = call(
        second_kernel,
        [like((8 * rows, 2 * share))] * n,
        *halves,
        w_fc2,
        w_fc2_other,
        scratch=[vmem((2, 8 * rows, out_cols), f32)],
        flops=32 * rows * w_fc2.size,
    )
    merged = [swap(merged[k], "hold", n, k) if k else merged[k] for k in range(n)]

    kept, sent = call(
        key_kernel,
        [like((4 * rows, n * key_cols + 128), f32), like((4 * rows, n * key_cols + 128))],
        *merged,
        key_mine,
        key_other,
        norm_gain,
        gain_other,
        scratch=[vmem((8 * rows, n * key_cols), f32)],
        flops=32 * rows * w_key.size,
    )
    keys = call(
        group_kernel,
        [like((rows, n * key_cols + 128), f32)] * n,
        kept,
        swap(sent, "tp", 2, 1),
        scratch=[vmem((4 * rows, n * key_cols + 128), f32)],
    )
    keys = [swap(keys[k], "hold", n, k) if k else keys[k] for k in range(n)]
    return call(
        functools.partial(last_kernel, width),
        like((1, rounds, block, n * key_cols)),
        *keys,
        matching,
    )


def per_device(cache, ln_gain, w_fc1, w_fc2, norm_gain, w_key, matching, counts):
    sizes = lax.axis_size("hold"), lax.axis_size("tp"), lax.axis_size("rep")
    rounds, block, depth = cache.shape[1:]
    group = sizes[1] * sizes[2]
    width = w_key.shape[0] * group
    few = sizes[0] * rounds * group * block <= w_fc1.shape[1]
    fits = sizes == (4, 2, 2) and rounds == 4 and block == 2
    plan = rows_past_weights if few and fits else rows_to_owners
    return plan(cache, ln_gain, w_fc1, w_fc2, norm_gain, w_key, matching, counts, width)


def solution(mesh):
    return jax.shard_map(
        per_device,
        mesh=mesh,
        in_specs=(
            P(("grp", "hold"), None, ("tp", "rep"), None),
            P(),
            P("hold", ("tp", "rep")),
            P("hold", ("tp", "rep")),
            P(("tp", "rep")),
            P(("tp", "rep"), "hold"),
            P("grp", None),
            P(("grp", "hold"), None, ("tp", "rep")),
        ),
        out_specs=P(("grp", "hold"), None, ("tp", "rep"), None),
        check_vma=False,
    )
```

```python
import functools

import jax
import jax.numpy as jnp
from jax import lax
from jax.experimental import pallas as pl
from jax.experimental.pallas import tpu as pltpu
from jax.sharding import PartitionSpec as P

EPSILON = 1e-06
GROUP_AXES = ("tp", "rep")
ALL_AXES = ("hold", "tp", "rep")


def patch_norm(rows, ln_gain):
    width = ln_gain.shape[0]
    patches = rows.astype(jnp.float32).reshape(rows.shape[0], -1, width)
    scale = lax.rsqrt(jnp.mean(patches * patches, axis=2, keepdims=True) + EPSILON)
    return patches * scale * ln_gain


def merger_features(rows, ln_gain, w_fc1, w_fc2, norm_gain, width):
    normed = patch_norm(rows, ln_gain).reshape(rows.shape[0], -1).astype(jnp.bfloat16)
    first_cols = lax.all_gather(w_fc1, "hold", axis=0, tiled=True)
    product = jnp.dot(
        lax.all_gather(normed, GROUP_AXES, axis=0, tiled=True),
        first_cols,
        preferred_element_type=jnp.float32,
    )
    hidden = jax.nn.gelu(product, approximate=False).astype(jnp.bfloat16)
    second_cols = lax.all_gather(w_fc2, "hold", axis=0, tiled=True)
    merged = jnp.dot(
        lax.all_gather(hidden, GROUP_AXES, axis=1, tiled=True),
        second_cols,
        preferred_element_type=jnp.float32,
    )
    squares = lax.psum(jnp.sum(merged * merged, axis=1), GROUP_AXES)
    scale = lax.rsqrt(squares / width + EPSILON)
    return (merged * scale[:, None] * norm_gain).astype(jnp.bfloat16)


def rows_to_owners(cache, ln_gain, w_fc1, w_fc2, norm_gain, w_key, matching, counts, width):
    rounds = cache.shape[1]
    block = cache.shape[2]
    holder_index = lax.axis_index("hold")
    owner_column = lax.dynamic_slice_in_dim(matching, holder_index, 1, 1)[:, 0]
    send_order = jnp.argsort(owner_column)
    source_of = jnp.argmax(matching == holder_index, axis=1)
    sent_counts = jnp.take(counts[0, :, 0], send_order)
    outgoing = jnp.take(cache[0], send_order, axis=0)
    arrived = lax.all_to_all(outgoing, "hold", split_axis=0, concat_axis=0, tiled=True)
    arrived_counts = lax.all_to_all(
        sent_counts.reshape(rounds, 1), "hold", split_axis=0, concat_axis=0, tiled=True
    )
    own_blocks = jnp.take(arrived, source_of, axis=0)
    own_counts = jnp.take(arrived_counts[:, 0], source_of)
    features = merger_features(
        own_blocks.reshape(rounds * block, -1), ln_gain, w_fc1, w_fc2, norm_gain, width
    )
    key_cols = lax.all_gather(w_key, "hold", axis=1, tiled=True)
    keys = lax.psum_scatter(
        jnp.dot(features, key_cols, preferred_element_type=jnp.float32),
        GROUP_AXES,
        scatter_dimension=0,
        tiled=True,
    )
    keys = keys.reshape(rounds, block, -1)
    valid = jnp.arange(block, dtype=jnp.int32)[None, :] < own_counts[:, None]
    keys = jnp.where(valid[:, :, None], keys, jnp.zeros_like(keys))
    return keys.astype(jnp.bfloat16)[None]


def swap(x, axis, n, step):
    return lax.ppermute(x, axis, [(i, i ^ step) for i in range(n)])


def exchange(parts):
    n = len(parts)
    return [swap(parts[k], "hold", n, k) for k in range(n - 1, 0, -1)] + [parts[0]]


def call(body, outs, *args, flops=0, scratch=(), **specs):
    moved = sum(x.size * x.dtype.itemsize for x in args)
    return pl.pallas_call(
        body,
        out_shape=outs,
        scratch_shapes=scratch,
        cost_estimate=pl.CostEstimate(flops=flops, bytes_accessed=moved, transcendentals=0),
        compiler_params=pltpu.CompilerParams(vmem_limit_bytes=16 << 20),
        **specs,
    )(*args)


def dot(a, b):
    return jnp.dot(a, b, preferred_element_type=jnp.float32)


def norm_rows(cache, gain, matching, held):
    h = lax.axis_index("hold")
    _, rounds, block, depth = cache.shape
    width = gain.shape[1]
    column = lax.broadcasted_iota(jnp.int32, matching.shape, 1) == h
    owner = jnp.sum(jnp.where(column, matching[...], 0), axis=1, keepdims=True)
    for p in range(depth // width):
        cols = pl.ds(p * width, width)
        normed = []
        for r in range(rounds):
            x = cache[0, r, :, cols].astype(jnp.float32)
            scale = lax.rsqrt(jnp.mean(x * x, axis=1, keepdims=True) + EPSILON)
            normed.append(x * scale * gain)
        for j in range(rounds):
            picked = sum(
                jnp.where(owner[r : r + 1] == j, normed[r], 0.0) for r in range(rounds)
            )
            held[j * block : (j + 1) * block, cols] = picked


def own_kernel(cache, ln_gain, matching, w_fc1, w_fc2, w_key, *refs):
    out, held_1, held_2, *key_rows = refs[:6]
    x_in, gain_in, plan_in, sems = refs[6:]
    h, grp = lax.axis_index("hold"), lax.axis_index("grp")
    pairs = [(cache, x_in), (ln_gain, gain_in), (matching, plan_in), (w_fc1, held_1), (w_fc2, held_2)]
    share = key_rows[0].shape[0]
    for place, end in zip((h, h ^ 1, h ^ 3 ^ grp), key_rows, strict=True):
        pairs.append((w_key.at[pl.ds(pl.multiple_of(place * share, 128), share)], end))
    copies = [pltpu.make_async_copy(a, b, sems.at[i]) for i, (a, b) in enumerate(pairs)]
    for copy in copies:
        copy.start()
    for copy in copies[:3]:
        copy.wait()
    norm_rows(x_in, gain_in[...].reshape(1, -1), plan_in, out)
    for copy in copies[3:]:
        copy.wait()


def both_kernel(own, cache, ln_gain, matching, *refs):
    outs, held = refs[:4], refs[4]
    h = lax.axis_index("hold")
    norm_rows(cache, ln_gain[...].reshape(1, -1), matching, held)
    chunk = outs[0].shape[1]
    for s, out in enumerate(outs):
        cols = pl.ds(pl.multiple_of((h ^ s) * chunk, 128), chunk)
        out[...] = jnp.concatenate([own[:, cols], held[:, cols]], axis=0).astype(jnp.bfloat16)


def first_kernel(*refs):
    pieces, weights, outs = refs[3::-1], refs[4:6], refs[6:10]
    rows, sums = refs[10:]
    h, rep = lax.axis_index("hold"), lax.axis_index("rep")
    size = pieces[0].shape[0] // 2
    half = 4 * size
    for k, piece in enumerate(pieces):
        part = piece[...].astype(jnp.float32)
        for b in range(2):
            start = pl.multiple_of(b * half + (h ^ k) * size, 8)
            rows[pl.ds(start, size), :] = part[b * size : (b + 1) * size]
    x = rows[...].astype(jnp.bfloat16)
    for i, weight in enumerate(weights):
        sums[rep ^ i] = dot(x, weight[...])
    for k, out in enumerate(outs):
        start = pl.multiple_of(((h ^ k) & 1) * half, 16)
        out[...] = sums[(h ^ k) >> 1, pl.ds(start, half), :].astype(jnp.bfloat16)


ERFC_NEAR = (
    2.326819970068386e-2,
    -1.387039388740657e-1,
    3.687424674597105e-1,
    -5.824733027278666e-1,
    6.210004621745983e-1,
    -4.944515323274145e-1,
    3.404879937665872e-1,
    -2.741127028184656e-1,
    5.638259427386472e-1,
)
ERFC_FAR = (
    -1.047766399936249e1,
    1.297719955372516e1,
    -7.495518717768503e0,
    2.921019019210786e0,
    -1.015265279202700e0,
    4.218463358204948e-1,
    -2.820767439740514e-1,
    5.641895067754075e-1,
)


def erfc(x):
    size = jnp.maximum(jnp.abs(x), 1.0)
    inverse = 1.0 / size
    square = inverse * inverse
    near, far = jnp.zeros_like(x), jnp.zeros_like(x)
    for c in ERFC_NEAR:
        near = near * square + c
    for c in ERFC_FAR:
        far = far * square + c
    tail = jnp.exp(-size * size) * inverse * jnp.where(size < 2.0, near, far)
    return jnp.where(jnp.abs(x) < 1.0, 1.0 - lax.erf(x), jnp.where(x < 0, 2.0 - tail, tail))


def gelu_kernel(*refs):
    x = sum(part[...].astype(jnp.float32) for part in refs[:4])
    refs[4][...] = (0.5 * x * erfc(-x * 0.5**0.5)).astype(jnp.bfloat16)


def second_kernel(first, second, w_mine, w_other, *refs):
    outs, sums = refs[:4], refs[4]
    h = lax.axis_index("hold")
    half = first.shape[0]
    bb = half // 16
    to = lax.broadcasted_iota(jnp.int32, (2 * half, half), 0)
    source = lax.broadcasted_iota(jnp.int32, (2 * half, half), 1)
    u, owner = to // half, (to % half) // (4 * bb)
    holder, b_of = (to % (4 * bb)) // bb, to % bb
    wanted = (u ^ (h >> 1)) * half + (holder * 4 + owner) * bb + b_of
    moved = 0.0
    for p, part in enumerate((first, second)):
        order = jnp.where(source + p * half == wanted, 1.0, 0.0)
        moved += dot(order.astype(jnp.bfloat16), part[...])
    moved = moved.astype(jnp.bfloat16)
    cols = outs[0].shape[1] // 2
    for p, weight in enumerate((w_mine, w_other)):
        sums[p] = dot(moved, weight[...])
        for k in range(4):
            start = pl.multiple_of((h ^ k) * cols, 128)
            part = sums[p, :, pl.ds(start, cols)].astype(jnp.bfloat16)
            outs[k][:, p * cols : (p + 1) * cols] = part


def two_terms(x):
    high = x.astype(jnp.bfloat16).astype(jnp.float32)
    lane = lax.broadcasted_iota(jnp.int32, (x.shape[0], 128), 1)
    return jnp.where(lane < 64, high, x - high)


def key_kernel(*refs):
    parts, blocks, gains = refs[:4], refs[4:6], refs[6:8]
    kept, sent, held = refs[8:]
    h, grp = lax.axis_index("hold"), lax.axis_index("grp")
    merged = sum(part[...].astype(jnp.float32) for part in parts)
    squares = jnp.sum(merged * merged, axis=1, keepdims=True)
    cols = merged.shape[1] // 2
    start = pl.multiple_of(h * cols, 128)
    rows = []
    for p in range(2):
        gain = gains[p][pl.ds(start, cols)].reshape(1, cols)
        rows.append((merged[:, p * cols : (p + 1) * cols] * gain).astype(jnp.bfloat16))
    width = blocks[0].shape[1]
    for i, place in enumerate((h, h ^ 1, h ^ 3 ^ grp, h ^ 2 ^ grp)):
        held[:, pl.ds(pl.multiple_of(place * width, 128), width)] = sum(
            dot(rows[p], blocks[p][i * cols : (i + 1) * cols, :]) for p in range(2)
        )
    half = kept.shape[0]
    keys = 4 * width
    kept[:, :keys] = held[:half, :]
    kept[:, keys:] = jnp.broadcast_to(squares[:half], (half, 128))
    sent[:, :keys] = held[half:, :].astype(jnp.bfloat16)
    sent[:, keys:] = two_terms(squares[half:]).astype(jnp.bfloat16)


def group_kernel(kept, came, matching, counts, *refs):
    outs, held = refs[:4], refs[4]
    h = lax.axis_index("hold")
    keys = kept.shape[1] - 128
    held[:, :keys] = kept[:, :keys] + came[:, :keys].astype(jnp.float32)
    pair = came[:, keys:].astype(jnp.float32)
    held[:, keys:] = two_terms(kept[:, keys : keys + 1] + pair[:, :1] + pair[:, 127:])
    rows = outs[0].shape[0]
    rounds = matching.shape[0]
    column = lax.broadcasted_iota(jnp.int32, matching.shape, 1) == h
    owner = jnp.sum(jnp.where(column, matching[...], 0), axis=1, keepdims=True)
    lane = lax.broadcasted_iota(jnp.int32, (rows, 128), 1)
    for k in range(4):
        part = held[pl.ds(pl.multiple_of((h ^ k) * rows, 8), rows), :]
        live = sum(
            jnp.where(owner[r : r + 1] == (h ^ k), counts[:, r : r + 1], 0) for r in range(rounds)
        )
        tail = jnp.where(lane == 32, live.astype(jnp.float32), part[:, keys:])
        outs[k][:, :keys] = part[:, :keys].astype(jnp.bfloat16)
        outs[k][:, keys:] = tail.astype(jnp.bfloat16)


def last_kernel(width, *refs):
    parts, matching, out, held = refs[3::-1], refs[4], refs[5], refs[6]
    h = lax.axis_index("hold")
    _, rounds, block, features = out.shape
    total = sum(part[...].astype(jnp.float32) for part in parts)
    squares = total[:, features : features + 1] + total[:, -1:]
    keys = total[:, :features] * lax.rsqrt(squares / width + EPSILON)
    for k, part in enumerate(parts):
        held[pl.ds(h ^ k, 1), :] = part[:1, features:].astype(jnp.float32)
    b_of = lax.broadcasted_iota(jnp.int32, (block, 1), 0).astype(jnp.float32)
    blocks = []
    for i in range(rounds):
        live = held[i : i + 1, 32:33]
        blocks.append(jnp.where(b_of < live, keys[i * block : (i + 1) * block], 0.0))
    for r in range(rounds):
        picked = sum(
            jnp.where(matching[r : r + 1, i : i + 1] == h, blocks[i], 0.0) for i in range(rounds)
        )
        out[0, r] = picked.astype(jnp.bfloat16)


def rows_past_weights(cache, ln_gain, w_fc1, w_fc2, norm_gain, w_key, matching, counts, width):
    n = lax.axis_size("hold")
    rounds, block, depth = cache.shape[1:]
    rows = rounds * block
    chunk = depth // n
    hidden_cols, out_cols, key_cols = w_fc1.shape[1], w_fc2.shape[1], w_key.shape[1]
    share = w_key.shape[0] // n
    f32, bf16 = jnp.float32, jnp.bfloat16
    vmem = pltpu.VMEM

    def like(dims, kind=bf16):
        return jax.ShapeDtypeStruct(dims, kind)

    cache_other = swap(cache, "tp", 2, 1)
    w_fc1_other = swap(w_fc1, "rep", 2, 1)
    gain_other = swap(norm_gain, "rep", 2, 1)
    cache_in, w_fc1_in, w_fc2_in, w_key_in, ln_in, matching_in = (
        pltpu.with_memory_space_constraint(x, pltpu.HBM)
        for x in (cache, w_fc1, w_fc2, w_key, ln_gain, matching)
    )
    own, w_fc1_mine, w_fc2_mine, key_0, key_1, key_far = call(
        own_kernel,
        [like((rows, depth), f32), like(w_fc1.shape), like(w_fc2.shape)]
        + [like((share, key_cols))] * 3,
        cache_in,
        ln_in,
        matching_in,
        w_fc1_in,
        w_fc2_in,
        w_key_in,
        in_specs=[pl.BlockSpec(memory_space=pltpu.HBM)] * 6,
        scratch=[
            vmem(cache.shape, bf16),
            vmem(ln_gain.shape, f32),
            vmem(matching.shape, jnp.int32),
            pltpu.SemaphoreType.DMA((8,)),
        ],
        flops=8 << 30,
    )
    key_1 = swap(key_1, "hold", n, 1)
    perm = [(n * g + a, n * g + (a ^ 3 ^ g)) for g in range(2) for a in range(n)]
    key_far = lax.ppermute(key_far, ("grp", "hold"), perm)
    own, cache_other, w_fc1_other, gain_other = lax.optimization_barrier(
        (own, cache_other, w_fc1_other, gain_other)
    )
    pieces = call(
        both_kernel,
        [like((2 * rows, chunk))] * n,
        own,
        cache_other,
        ln_gain,
        matching,
        scratch=[vmem((rows, depth), f32)],
        flops=8 << 30,
    )
    pieces = exchange(pieces)
    partial = call(
        first_kernel,
        [like((4 * rows, hidden_cols))] * n,
        *pieces,
        w_fc1_mine,
        w_fc1_other,
        scratch=[vmem((8 * rows, chunk), f32), vmem((2, 8 * rows, hidden_cols), f32)],
        flops=32 * rows * w_fc1.size,
    )
    *partial, key_1, key_far, w_fc2_sent = lax.optimization_barrier(
        (*partial, key_1, key_far, w_fc2_mine)
    )
    w_fc2_other = swap(w_fc2_sent, "rep", 2, 1)
    parts = exchange(partial)
    key_near = swap(key_far, "grp", 2, 1)
    hidden = call(gelu_kernel, like(parts[0].shape), *parts, flops=8 << 30)

    halves = []
    for g in range(2):
        perm = [
            (2 * a + b, 2 * (2 * b + (a >> 1)) + ((a & 1) ^ g)) for a in range(n) for b in range(2)
        ]
        halves.append(lax.ppermute(hidden, ("hold", "tp"), perm))

    merged = call(
        second_kernel,
        [like((8 * rows, 2 * share))] * n,
        *halves,
        w_fc2_mine,
        w_fc2_other,
        scratch=[vmem((2, 8 * rows, out_cols), f32)],
        flops=32 * rows * w_fc2.size,
    )
    *merged, key_near = lax.optimization_barrier((*merged, key_near))
    key_mine = jnp.concatenate([key_0, key_1, key_far, key_near])
    key_other = swap(key_mine, "rep", 2, 1)
    merged = exchange(merged)
    kept, sent = call(
        key_kernel,
        [like((4 * rows, n * key_cols + 128), f32), like((4 * rows, n * key_cols + 128))],
        *merged,
        key_mine,
        key_other,
        norm_gain,
        gain_other,
        scratch=[vmem((8 * rows, n * key_cols), f32)],
        flops=32 * rows * w_key.size,
    )
    keys = call(
        group_kernel,
        [like((rows, n * key_cols + 128))] * n,
        kept,
        swap(sent, "tp", 2, 1),
        matching,
        counts.reshape(1, rounds),
        scratch=[vmem((4 * rows, n * key_cols + 128), f32)],
    )
    keys = exchange(keys)
    return call(
        functools.partial(last_kernel, width),
        like((1, rounds, block, n * key_cols)),
        *keys,
        matching,
        scratch=[vmem((rounds, 128), f32)],
    )


def per_device(cache, ln_gain, w_fc1, w_fc2, norm_gain, w_key, matching, counts):
    sizes = lax.axis_size("hold"), lax.axis_size("tp"), lax.axis_size("rep")
    rounds, block, depth = cache.shape[1:]
    group = sizes[1] * sizes[2]
    width = w_key.shape[0] * group
    few = sizes[0] * rounds * group * block <= w_fc1.shape[1]
    fits = sizes == (4, 2, 2) and rounds == 4 and block == 2
    plan = rows_past_weights if few and fits else rows_to_owners
    return plan(cache, ln_gain, w_fc1, w_fc2, norm_gain, w_key, matching, counts, width)


def solution(mesh):
    return jax.shard_map(
        per_device,
        mesh=mesh,
        in_specs=(
            P(("grp", "hold"), None, ("tp", "rep"), None),
            P(),
            P("hold", ("tp", "rep")),
            P("hold", ("tp", "rep")),
            P(("tp", "rep")),
            P(("tp", "rep"), "hold"),
            P("grp", None),
            P(("grp", "hold"), None, ("tp", "rep")),
        ),
        out_specs=P(("grp", "hold"), None, ("tp", "rep"), None),
        check_vma=False,
    )
```

```python
import functools

import jax
import jax.numpy as jnp
from jax import lax
from jax.experimental import pallas as pl
from jax.experimental.pallas import tpu as pltpu
from jax.sharding import PartitionSpec as P

EPSILON = 1e-06
GROUP_AXES = ("tp", "rep")
ALL_AXES = ("hold", "tp", "rep")


def patch_norm(rows, ln_gain):
    width = ln_gain.shape[0]
    patches = rows.astype(jnp.float32).reshape(rows.shape[0], -1, width)
    scale = lax.rsqrt(jnp.mean(patches * patches, axis=2, keepdims=True) + EPSILON)
    return patches * scale * ln_gain


def merger_features(rows, ln_gain, w_fc1, w_fc2, norm_gain, width):
    normed = patch_norm(rows, ln_gain).reshape(rows.shape[0], -1).astype(jnp.bfloat16)
    first_cols = lax.all_gather(w_fc1, "hold", axis=0, tiled=True)
    product = jnp.dot(
        lax.all_gather(normed, GROUP_AXES, axis=0, tiled=True),
        first_cols,
        preferred_element_type=jnp.float32,
    )
    hidden = jax.nn.gelu(product, approximate=False).astype(jnp.bfloat16)
    second_cols = lax.all_gather(w_fc2, "hold", axis=0, tiled=True)
    merged = jnp.dot(
        lax.all_gather(hidden, GROUP_AXES, axis=1, tiled=True),
        second_cols,
        preferred_element_type=jnp.float32,
    )
    squares = lax.psum(jnp.sum(merged * merged, axis=1), GROUP_AXES)
    scale = lax.rsqrt(squares / width + EPSILON)
    return (merged * scale[:, None] * norm_gain).astype(jnp.bfloat16)


def rows_to_owners(cache, ln_gain, w_fc1, w_fc2, norm_gain, w_key, matching, counts, width):
    rounds = cache.shape[1]
    block = cache.shape[2]
    holder_index = lax.axis_index("hold")
    owner_column = lax.dynamic_slice_in_dim(matching, holder_index, 1, 1)[:, 0]
    send_order = jnp.argsort(owner_column)
    source_of = jnp.argmax(matching == holder_index, axis=1)
    sent_counts = jnp.take(counts[0, :, 0], send_order)
    outgoing = jnp.take(cache[0], send_order, axis=0)
    arrived = lax.all_to_all(outgoing, "hold", split_axis=0, concat_axis=0, tiled=True)
    arrived_counts = lax.all_to_all(
        sent_counts.reshape(rounds, 1), "hold", split_axis=0, concat_axis=0, tiled=True
    )
    own_blocks = jnp.take(arrived, source_of, axis=0)
    own_counts = jnp.take(arrived_counts[:, 0], source_of)
    features = merger_features(
        own_blocks.reshape(rounds * block, -1), ln_gain, w_fc1, w_fc2, norm_gain, width
    )
    key_cols = lax.all_gather(w_key, "hold", axis=1, tiled=True)
    keys = lax.psum_scatter(
        jnp.dot(features, key_cols, preferred_element_type=jnp.float32),
        GROUP_AXES,
        scatter_dimension=0,
        tiled=True,
    )
    keys = keys.reshape(rounds, block, -1)
    valid = jnp.arange(block, dtype=jnp.int32)[None, :] < own_counts[:, None]
    keys = jnp.where(valid[:, :, None], keys, jnp.zeros_like(keys))
    return keys.astype(jnp.bfloat16)[None]


def swap(x, axis, n, step):
    return lax.ppermute(x, axis, [(i, i ^ step) for i in range(n)])


def exchange(parts, order):
    n = len(parts)
    return [swap(parts[k], "hold", n, k) for k in order] + [parts[0]]


def call(body, outs, *args, flops=0, scratch=(), **specs):
    moved = sum(x.size * x.dtype.itemsize for x in args)
    return pl.pallas_call(
        body,
        out_shape=outs,
        scratch_shapes=scratch,
        cost_estimate=pl.CostEstimate(flops=flops, bytes_accessed=moved, transcendentals=0),
        compiler_params=pltpu.CompilerParams(vmem_limit_bytes=16 << 20),
        **specs,
    )(*args)


def dot(a, b):
    return jnp.dot(a, b, preferred_element_type=jnp.float32)


def norm_rows(cache, gain, matching, held):
    h = lax.axis_index("hold")
    _, rounds, block, depth = cache.shape
    width = gain.shape[1]
    column = lax.broadcasted_iota(jnp.int32, matching.shape, 1) == h
    owner = jnp.sum(jnp.where(column, matching[...], 0), axis=1, keepdims=True)
    for p in range(depth // width):
        cols = pl.ds(p * width, width)
        normed = []
        for r in range(rounds):
            x = cache[0, r, :, cols].astype(jnp.float32)
            scale = lax.rsqrt(jnp.mean(x * x, axis=1, keepdims=True) + EPSILON)
            normed.append(x * scale * gain)
        for j in range(rounds):
            picked = sum(
                jnp.where(owner[r : r + 1] == j, normed[r], 0.0) for r in range(rounds)
            )
            held[j * block : (j + 1) * block, cols] = picked


def own_kernel(cache, ln_gain, matching, w_fc1, w_fc2, w_key, *refs):
    out, held_1, held_2, *key_rows = refs[:6]
    x_in, gain_in, plan_in, sems = refs[6:]
    h, grp = lax.axis_index("hold"), lax.axis_index("grp")
    pairs = [(cache, x_in), (ln_gain, gain_in), (matching, plan_in), (w_fc1, held_1), (w_fc2, held_2)]
    share = key_rows[0].shape[0]
    for place, end in zip((h, h ^ 1, h ^ 3 ^ grp), key_rows, strict=True):
        pairs.append((w_key.at[pl.ds(pl.multiple_of(place * share, 128), share)], end))
    copies = [pltpu.make_async_copy(a, b, sems.at[i]) for i, (a, b) in enumerate(pairs)]
    for copy in copies:
        copy.start()
    for copy in copies[:3]:
        copy.wait()
    norm_rows(x_in, gain_in[...].reshape(1, -1), plan_in, out)
    for copy in copies[3:]:
        copy.wait()


def both_kernel(own, cache, ln_gain, matching, *refs):
    outs, held = refs[:4], refs[4]
    h = lax.axis_index("hold")
    norm_rows(cache, ln_gain[...].reshape(1, -1), matching, held)
    chunk = outs[0].shape[1]
    for s, out in enumerate(outs):
        cols = pl.ds(pl.multiple_of((h ^ s) * chunk, 128), chunk)
        out[...] = jnp.concatenate([own[:, cols], held[:, cols]], axis=0).astype(jnp.bfloat16)


def first_kernel(places, *refs):
    pieces, weights, outs = refs[:4], refs[4:6], refs[6:10]
    rows, sums = refs[10:]
    h, rep = lax.axis_index("hold"), lax.axis_index("rep")
    size = pieces[0].shape[0] // 2
    half = 4 * size
    for k, piece in zip((*places, 0), pieces, strict=True):
        part = piece[...].astype(jnp.float32)
        for b in range(2):
            start = pl.multiple_of(b * half + (h ^ k) * size, 8)
            rows[pl.ds(start, size), :] = part[b * size : (b + 1) * size]
    x = rows[...].astype(jnp.bfloat16)
    for i, weight in enumerate(weights):
        sums[rep ^ i] = dot(x, weight[...])
    for k, out in enumerate(outs):
        start = pl.multiple_of(((h ^ k) & 1) * half, 16)
        out[...] = sums[(h ^ k) >> 1, pl.ds(start, half), :].astype(jnp.bfloat16)


ERFC_NEAR = (
    2.326819970068386e-2,
    -1.387039388740657e-1,
    3.687424674597105e-1,
    -5.824733027278666e-1,
    6.210004621745983e-1,
    -4.944515323274145e-1,
    3.404879937665872e-1,
    -2.741127028184656e-1,
    5.638259427386472e-1,
)
ERFC_FAR = (
    -1.047766399936249e1,
    1.297719955372516e1,
    -7.495518717768503e0,
    2.921019019210786e0,
    -1.015265279202700e0,
    4.218463358204948e-1,
    -2.820767439740514e-1,
    5.641895067754075e-1,
)


def erfc(x):
    size = jnp.maximum(jnp.abs(x), 1.0)
    inverse = 1.0 / size
    square = inverse * inverse
    near, far = jnp.zeros_like(x), jnp.zeros_like(x)
    for c in ERFC_NEAR:
        near = near * square + c
    for c in ERFC_FAR:
        far = far * square + c
    tail = jnp.exp(-size * size) * inverse * jnp.where(size < 2.0, near, far)
    return jnp.where(jnp.abs(x) < 1.0, 1.0 - lax.erf(x), jnp.where(x < 0, 2.0 - tail, tail))


def gelu_kernel(*refs):
    x = sum(part[...].astype(jnp.float32) for part in refs[:4])
    refs[4][...] = (0.5 * x * erfc(-x * 0.5**0.5)).astype(jnp.bfloat16)


def second_kernel(first, second, w_mine, w_other, *refs):
    outs, sums = refs[:4], refs[4]
    h = lax.axis_index("hold")
    half = first.shape[0]
    bb = half // 16
    to = lax.broadcasted_iota(jnp.int32, (2 * half, half), 0)
    source = lax.broadcasted_iota(jnp.int32, (2 * half, half), 1)
    u, owner = to // half, (to % half) // (4 * bb)
    holder, b_of = (to % (4 * bb)) // bb, to % bb
    wanted = (u ^ (h >> 1)) * half + (holder * 4 + owner) * bb + b_of
    moved = 0.0
    for p, part in enumerate((first, second)):
        order = jnp.where(source + p * half == wanted, 1.0, 0.0)
        moved += dot(order.astype(jnp.bfloat16), part[...])
    moved = moved.astype(jnp.bfloat16)
    cols = outs[0].shape[1] // 2
    for p, weight in enumerate((w_mine, w_other)):
        sums[p] = dot(moved, weight[...])
        for k in range(4):
            start = pl.multiple_of((h ^ k) * cols, 128)
            part = sums[p, :, pl.ds(start, cols)].astype(jnp.bfloat16)
            outs[k][:, p * cols : (p + 1) * cols] = part


def two_terms(x):
    high = x.astype(jnp.bfloat16).astype(jnp.float32)
    lane = lax.broadcasted_iota(jnp.int32, (x.shape[0], 128), 1)
    return jnp.where(lane < 64, high, x - high)


def key_kernel(*refs):
    parts, blocks, gains = refs[:4], refs[4:6], refs[6:8]
    kept, sent, held = refs[8:]
    h, grp = lax.axis_index("hold"), lax.axis_index("grp")
    merged = sum(part[...].astype(jnp.float32) for part in parts)
    squares = jnp.sum(merged * merged, axis=1, keepdims=True)
    cols = merged.shape[1] // 2
    start = pl.multiple_of(h * cols, 128)
    rows = []
    for p in range(2):
        gain = gains[p][pl.ds(start, cols)].reshape(1, cols)
        rows.append((merged[:, p * cols : (p + 1) * cols] * gain).astype(jnp.bfloat16))
    width = blocks[0].shape[1]
    for i, place in enumerate((h, h ^ 1, h ^ 3 ^ grp, h ^ 2 ^ grp)):
        held[:, pl.ds(pl.multiple_of(place * width, 128), width)] = sum(
            dot(rows[p], blocks[p][i * cols : (i + 1) * cols, :]) for p in range(2)
        )
    half = kept.shape[0]
    keys = 4 * width
    kept[:, :keys] = held[:half, :]
    kept[:, keys:] = jnp.broadcast_to(squares[:half], (half, 128))
    sent[:, :keys] = held[half:, :].astype(jnp.bfloat16)
    sent[:, keys:] = two_terms(squares[half:]).astype(jnp.bfloat16)


def group_kernel(kept, came, matching, counts, *refs):
    outs, held = refs[:4], refs[4]
    h = lax.axis_index("hold")
    keys = kept.shape[1] - 128
    held[:, :keys] = kept[:, :keys] + came[:, :keys].astype(jnp.float32)
    pair = came[:, keys:].astype(jnp.float32)
    held[:, keys:] = two_terms(kept[:, keys : keys + 1] + pair[:, :1] + pair[:, 127:])
    rows = outs[0].shape[0]
    rounds = matching.shape[0]
    column = lax.broadcasted_iota(jnp.int32, matching.shape, 1) == h
    owner = jnp.sum(jnp.where(column, matching[...], 0), axis=1, keepdims=True)
    lane = lax.broadcasted_iota(jnp.int32, (rows, 128), 1)
    for k in range(4):
        part = held[pl.ds(pl.multiple_of((h ^ k) * rows, 8), rows), :]
        live = sum(
            jnp.where(owner[r : r + 1] == (h ^ k), counts[:, r : r + 1], 0) for r in range(rounds)
        )
        tail = jnp.where(lane == 32, live.astype(jnp.float32), part[:, keys:])
        outs[k][:, :keys] = part[:, :keys].astype(jnp.bfloat16)
        outs[k][:, keys:] = tail.astype(jnp.bfloat16)


def last_kernel(width, places, *refs):
    parts, matching, out, held = refs[:4], refs[4], refs[5], refs[6]
    h = lax.axis_index("hold")
    _, rounds, block, features = out.shape
    total = sum(part[...].astype(jnp.float32) for part in parts)
    squares = total[:, features : features + 1] + total[:, -1:]
    keys = total[:, :features] * lax.rsqrt(squares / width + EPSILON)
    for k, part in zip((*places, 0), parts, strict=True):
        held[pl.ds(h ^ k, 1), :] = part[:1, features:].astype(jnp.float32)
    b_of = lax.broadcasted_iota(jnp.int32, (block, 1), 0).astype(jnp.float32)
    blocks = []
    for i in range(rounds):
        live = held[i : i + 1, 32:33]
        blocks.append(jnp.where(b_of < live, keys[i * block : (i + 1) * block], 0.0))
    for r in range(rounds):
        picked = sum(
            jnp.where(matching[r : r + 1, i : i + 1] == h, blocks[i], 0.0) for i in range(rounds)
        )
        out[0, r] = picked.astype(jnp.bfloat16)


def rows_past_weights(cache, ln_gain, w_fc1, w_fc2, norm_gain, w_key, matching, counts, width):
    n = lax.axis_size("hold")
    rounds, block, depth = cache.shape[1:]
    rows = rounds * block
    chunk = depth // n
    hidden_cols, out_cols, key_cols = w_fc1.shape[1], w_fc2.shape[1], w_key.shape[1]
    share = w_key.shape[0] // n
    f32, bf16 = jnp.float32, jnp.bfloat16
    vmem = pltpu.VMEM

    def like(dims, kind=bf16):
        return jax.ShapeDtypeStruct(dims, kind)

    long = 8 << 30
    hbm = pl.BlockSpec(memory_space=pltpu.HBM)
    in_hbm = [
        pltpu.with_memory_space_constraint(x, pltpu.HBM)
        for x in (cache, ln_gain, matching, w_fc1, w_fc2, w_key)
    ]
    cache_other = swap(cache, "tp", 2, 1)
    own, w_fc1_mine, w_fc2_mine, key_0, key_1, key_far = call(
        own_kernel,
        [like((rows, depth), f32), like(w_fc1.shape), like(w_fc2.shape)]
        + [like((share, key_cols))] * 3,
        *in_hbm,
        in_specs=[hbm] * 6,
        scratch=[
            vmem(cache.shape, bf16),
            vmem(ln_gain.shape, f32),
            vmem(matching.shape, jnp.int32),
            pltpu.SemaphoreType.DMA((8,)),
        ],
        flops=long,
    )
    w_fc1_other = swap(w_fc1, "rep", 2, 1)
    gain_other = swap(norm_gain, "rep", 2, 1)
    own, cache_other, w_fc2_sent, gain_other = lax.optimization_barrier(
        (own, cache_other, w_fc2_mine, gain_other)
    )
    w_fc2_other = swap(w_fc2_sent, "rep", 2, 1)
    pieces = call(
        both_kernel,
        [like((2 * rows, chunk))] * n,
        own,
        cache_other,
        ln_gain,
        matching,
        scratch=[vmem((rows, depth), f32)],
        flops=long,
    )

    *pieces, key_1, key_far = lax.optimization_barrier((*pieces, key_1, key_far))
    key_1 = swap(key_1, "hold", n, 1)
    perm = [(n * g + a, n * g + (a ^ 3 ^ g)) for g in range(2) for a in range(n)]
    key_far = lax.ppermute(key_far, ("grp", "hold"), perm)

    order = (3, 2, 1)
    partial = call(
        functools.partial(first_kernel, order),
        [like((4 * rows, hidden_cols))] * n,
        *exchange(pieces, order),
        w_fc1_mine,
        w_fc1_other,
        scratch=[vmem((8 * rows, chunk), f32), vmem((2, 8 * rows, hidden_cols), f32)],
        flops=long,
    )
    *partial, w_fc2_other = lax.optimization_barrier((*partial, w_fc2_other))
    key_near = swap(key_far, "grp", 2, 1)
    parts = exchange(partial, (1, 3, 2))
    hidden = call(gelu_kernel, like(parts[0].shape), *parts)

    halves = []
    for g in range(2):
        perm = [
            (2 * a + b, 2 * (2 * b + (a >> 1)) + ((a & 1) ^ g)) for a in range(n) for b in range(2)
        ]
        halves.append(lax.ppermute(hidden, ("hold", "tp"), perm))
    *halves, key_1 = lax.optimization_barrier((*halves, key_1))
    merged = call(
        second_kernel,
        [like((8 * rows, 2 * share))] * n,
        *halves,
        w_fc2_mine,
        w_fc2_other,
        scratch=[vmem((2, 8 * rows, out_cols), f32)],
        flops=32 * rows * w_fc2.size,
    )
    *merged, key_near = lax.optimization_barrier((*merged, key_near))
    key_mine = jnp.concatenate([key_0, key_1, key_far, key_near])
    key_other = swap(key_mine, "rep", 2, 1)
    kept, sent = call(
        key_kernel,
        [like((4 * rows, n * key_cols + 128), f32), like((4 * rows, n * key_cols + 128))],
        *exchange(merged, (2, 1, 3)),
        key_mine,
        key_other,
        norm_gain,
        gain_other,
        scratch=[vmem((8 * rows, n * key_cols), f32)],
        flops=32 * rows * w_key.size,
    )
    keys = call(
        group_kernel,
        [like((rows, n * key_cols + 128))] * n,
        kept,
        swap(sent, "tp", 2, 1),
        matching,
        counts.reshape(1, rounds),
        scratch=[vmem((4 * rows, n * key_cols + 128), f32)],
    )
    order = (3, 2, 1)
    return call(
        functools.partial(last_kernel, width, order),
        like((1, rounds, block, n * key_cols)),
        *exchange(keys, order),
        matching,
        scratch=[vmem((rounds, 128), f32)],
    )


def per_device(cache, ln_gain, w_fc1, w_fc2, norm_gain, w_key, matching, counts):
    sizes = lax.axis_size("hold"), lax.axis_size("tp"), lax.axis_size("rep")
    rounds, block, depth = cache.shape[1:]
    group = sizes[1] * sizes[2]
    width = w_key.shape[0] * group
    few = sizes[0] * rounds * group * block <= w_fc1.shape[1]
    fits = sizes == (4, 2, 2) and rounds == 4 and block == 2
    plan = rows_past_weights if few and fits else rows_to_owners
    return plan(cache, ln_gain, w_fc1, w_fc2, norm_gain, w_key, matching, counts, width)


def solution(mesh):
    return jax.shard_map(
        per_device,
        mesh=mesh,
        in_specs=(
            P(("grp", "hold"), None, ("tp", "rep"), None),
            P(),
            P("hold", ("tp", "rep")),
            P("hold", ("tp", "rep")),
            P(("tp", "rep")),
            P(("tp", "rep"), "hold"),
            P("grp", None),
            P(("grp", "hold"), None, ("tp", "rep")),
        ),
        out_specs=P(("grp", "hold"), None, ("tp", "rep"), None),
        check_vma=False,
    )
```

```python
import functools

import jax
import jax.numpy as jnp
from jax import lax
from jax.experimental import pallas as pl
from jax.experimental.pallas import tpu as pltpu
from jax.sharding import PartitionSpec as P

EPSILON = 1e-06
GROUP_AXES = ("tp", "rep")
ALL_AXES = ("hold", "tp", "rep")


def patch_norm(rows, ln_gain):
    width = ln_gain.shape[0]
    patches = rows.astype(jnp.float32).reshape(rows.shape[0], -1, width)
    scale = lax.rsqrt(jnp.mean(patches * patches, axis=2, keepdims=True) + EPSILON)
    return patches * scale * ln_gain


def merger_features(rows, ln_gain, w_fc1, w_fc2, norm_gain, width):
    normed = patch_norm(rows, ln_gain).reshape(rows.shape[0], -1).astype(jnp.bfloat16)
    first_cols = lax.all_gather(w_fc1, "hold", axis=0, tiled=True)
    product = jnp.dot(
        lax.all_gather(normed, GROUP_AXES, axis=0, tiled=True),
        first_cols,
        preferred_element_type=jnp.float32,
    )
    hidden = jax.nn.gelu(product, approximate=False).astype(jnp.bfloat16)
    second_cols = lax.all_gather(w_fc2, "hold", axis=0, tiled=True)
    merged = jnp.dot(
        lax.all_gather(hidden, GROUP_AXES, axis=1, tiled=True),
        second_cols,
        preferred_element_type=jnp.float32,
    )
    squares = lax.psum(jnp.sum(merged * merged, axis=1), GROUP_AXES)
    scale = lax.rsqrt(squares / width + EPSILON)
    return (merged * scale[:, None] * norm_gain).astype(jnp.bfloat16)


def rows_to_owners(cache, ln_gain, w_fc1, w_fc2, norm_gain, w_key, matching, counts, width):
    rounds = cache.shape[1]
    block = cache.shape[2]
    holder_index = lax.axis_index("hold")
    owner_column = lax.dynamic_slice_in_dim(matching, holder_index, 1, 1)[:, 0]
    send_order = jnp.argsort(owner_column)
    source_of = jnp.argmax(matching == holder_index, axis=1)
    sent_counts = jnp.take(counts[0, :, 0], send_order)
    outgoing = jnp.take(cache[0], send_order, axis=0)
    arrived = lax.all_to_all(outgoing, "hold", split_axis=0, concat_axis=0, tiled=True)
    arrived_counts = lax.all_to_all(
        sent_counts.reshape(rounds, 1), "hold", split_axis=0, concat_axis=0, tiled=True
    )
    own_blocks = jnp.take(arrived, source_of, axis=0)
    own_counts = jnp.take(arrived_counts[:, 0], source_of)
    features = merger_features(
        own_blocks.reshape(rounds * block, -1), ln_gain, w_fc1, w_fc2, norm_gain, width
    )
    key_cols = lax.all_gather(w_key, "hold", axis=1, tiled=True)
    keys = lax.psum_scatter(
        jnp.dot(features, key_cols, preferred_element_type=jnp.float32),
        GROUP_AXES,
        scatter_dimension=0,
        tiled=True,
    )
    keys = keys.reshape(rounds, block, -1)
    valid = jnp.arange(block, dtype=jnp.int32)[None, :] < own_counts[:, None]
    keys = jnp.where(valid[:, :, None], keys, jnp.zeros_like(keys))
    return keys.astype(jnp.bfloat16)[None]


def swap(x, axis, n, step):
    return lax.ppermute(x, axis, [(i, i ^ step) for i in range(n)])


def exchange(parts, order):
    n = len(parts)
    return [swap(parts[k], "hold", n, k) for k in order] + [parts[0]]


def call(body, outs, *args, flops=0, scratch=(), **specs):
    moved = sum(x.size * x.dtype.itemsize for x in args)
    return pl.pallas_call(
        body,
        out_shape=outs,
        scratch_shapes=scratch,
        cost_estimate=pl.CostEstimate(flops=flops, bytes_accessed=moved, transcendentals=0),
        compiler_params=pltpu.CompilerParams(vmem_limit_bytes=16 << 20),
        **specs,
    )(*args)


def dot(a, b):
    return jnp.dot(a, b, preferred_element_type=jnp.float32)


def norm_rows(cache, gain, matching, held):
    h = lax.axis_index("hold")
    _, rounds, block, depth = cache.shape
    width = gain.shape[1]
    column = lax.broadcasted_iota(jnp.int32, matching.shape, 1) == h
    owner = jnp.sum(jnp.where(column, matching[...], 0), axis=1, keepdims=True)
    for p in range(depth // width):
        cols = pl.ds(p * width, width)
        normed = []
        for r in range(rounds):
            x = cache[0, r, :, cols].astype(jnp.float32)
            scale = lax.rsqrt(jnp.mean(x * x, axis=1, keepdims=True) + EPSILON)
            normed.append(x * scale * gain)
        for j in range(rounds):
            picked = sum(
                jnp.where(owner[r : r + 1] == j, normed[r], 0.0) for r in range(rounds)
            )
            held[j * block : (j + 1) * block, cols] = picked


def own_kernel(cache, ln_gain, matching, w_fc1, w_fc2, w_key, *refs):
    out, held_1, held_2, *key_rows = refs[:6]
    x_in, gain_in, plan_in, sems = refs[6:]
    h, grp = lax.axis_index("hold"), lax.axis_index("grp")
    pairs = [(cache, x_in), (ln_gain, gain_in), (matching, plan_in), (w_fc1, held_1), (w_fc2, held_2)]
    share = key_rows[0].shape[0]
    for place, end in zip((h, h ^ 1, h ^ 3 ^ grp), key_rows, strict=True):
        pairs.append((w_key.at[pl.ds(pl.multiple_of(place * share, 128), share)], end))
    copies = [pltpu.make_async_copy(a, b, sems.at[i]) for i, (a, b) in enumerate(pairs)]
    for copy in copies:
        copy.start()
    for copy in copies[:3]:
        copy.wait()
    norm_rows(x_in, gain_in[...].reshape(1, -1), plan_in, out)
    for copy in copies[3:]:
        copy.wait()


def both_kernel(own, cache, ln_gain, matching, *refs):
    outs, held = refs[:4], refs[4]
    h = lax.axis_index("hold")
    norm_rows(cache, ln_gain[...].reshape(1, -1), matching, held)
    chunk = outs[0].shape[1]
    for s, out in enumerate(outs):
        cols = pl.ds(pl.multiple_of((h ^ s) * chunk, 128), chunk)
        out[...] = jnp.concatenate([own[:, cols], held[:, cols]], axis=0).astype(jnp.bfloat16)


def first_kernel(places, *refs):
    pieces, weights, outs = refs[:4], refs[4:6], refs[6:10]
    rows, sums = refs[10:]
    h, rep = lax.axis_index("hold"), lax.axis_index("rep")
    size = pieces[0].shape[0] // 2
    half = 4 * size
    for k, piece in zip((*places, 0), pieces, strict=True):
        part = piece[...].astype(jnp.float32)
        for b in range(2):
            start = pl.multiple_of(b * half + (h ^ k) * size, 8)
            rows[pl.ds(start, size), :] = part[b * size : (b + 1) * size]
    x = rows[...].astype(jnp.bfloat16)
    for i, weight in enumerate(weights):
        sums[rep ^ i] = dot(x, weight[...])
    for k, out in enumerate(outs):
        start = pl.multiple_of(((h ^ k) & 1) * half, 16)
        out[...] = sums[(h ^ k) >> 1, pl.ds(start, half), :].astype(jnp.bfloat16)


ERFC_NEAR = (
    2.326819970068386e-2,
    -1.387039388740657e-1,
    3.687424674597105e-1,
    -5.824733027278666e-1,
    6.210004621745983e-1,
    -4.944515323274145e-1,
    3.404879937665872e-1,
    -2.741127028184656e-1,
    5.638259427386472e-1,
)
ERFC_FAR = (
    -1.047766399936249e1,
    1.297719955372516e1,
    -7.495518717768503e0,
    2.921019019210786e0,
    -1.015265279202700e0,
    4.218463358204948e-1,
    -2.820767439740514e-1,
    5.641895067754075e-1,
)


def erfc(x):
    size = jnp.maximum(jnp.abs(x), 1.0)
    inverse = 1.0 / size
    square = inverse * inverse
    near, far = jnp.zeros_like(x), jnp.zeros_like(x)
    for c in ERFC_NEAR:
        near = near * square + c
    for c in ERFC_FAR:
        far = far * square + c
    tail = jnp.exp(-size * size) * inverse * jnp.where(size < 2.0, near, far)
    return jnp.where(jnp.abs(x) < 1.0, 1.0 - lax.erf(x), jnp.where(x < 0, 2.0 - tail, tail))


def gelu_kernel(*refs):
    x = sum(part[...].astype(jnp.float32) for part in refs[:4])
    refs[4][...] = (0.5 * x * erfc(-x * 0.5**0.5)).astype(jnp.bfloat16)


def second_kernel(first, second, w_mine, w_other, *refs):
    outs, sums = refs[:4], refs[4]
    h = lax.axis_index("hold")
    half = first.shape[0]
    bb = half // 16
    to = lax.broadcasted_iota(jnp.int32, (2 * half, half), 0)
    source = lax.broadcasted_iota(jnp.int32, (2 * half, half), 1)
    u, owner = to // half, (to % half) // (4 * bb)
    holder, b_of = (to % (4 * bb)) // bb, to % bb
    wanted = (u ^ (h & 1)) * half + (holder * 4 + owner) * bb + b_of
    moved = 0.0
    for p, part in enumerate((first, second)):
        order = jnp.where(source + p * half == wanted, 1.0, 0.0)
        moved += dot(order.astype(jnp.bfloat16), part[...])
    moved = moved.astype(jnp.bfloat16)
    cols = outs[0].shape[1] // 2
    for p, weight in enumerate((w_mine, w_other)):
        sums[p] = dot(moved, weight[...])
        for k in range(4):
            start = pl.multiple_of((h ^ k) * cols, 128)
            part = sums[p, :, pl.ds(start, cols)].astype(jnp.bfloat16)
            outs[k][:, p * cols : (p + 1) * cols] = part


def two_terms(x):
    high = x.astype(jnp.bfloat16).astype(jnp.float32)
    lane = lax.broadcasted_iota(jnp.int32, (x.shape[0], 128), 1)
    return jnp.where(lane < 64, high, x - high)


def key_kernel(*refs):
    parts, blocks, gains, matching, counts = refs[:4], refs[4:6], refs[6:8], refs[8], refs[9]
    outs, held = refs[10:14], refs[14]
    h, grp = lax.axis_index("hold"), lax.axis_index("grp")
    merged = sum(part[...].astype(jnp.float32) for part in parts)
    squares = jnp.sum(merged * merged, axis=1, keepdims=True)
    cols = merged.shape[1] // 2
    start = pl.multiple_of(h * cols, 128)
    rows = []
    for p in range(2):
        gain = gains[p][pl.ds(start, cols)].reshape(1, cols)
        rows.append((merged[:, p * cols : (p + 1) * cols] * gain).astype(jnp.bfloat16))
    width = blocks[0].shape[1]
    for i, place in enumerate((h, h ^ 1, h ^ 3 ^ grp, h ^ 2 ^ grp)):
        held[:, pl.ds(pl.multiple_of(place * width, 128), width)] = sum(
            dot(rows[p], blocks[p][i * cols : (i + 1) * cols, :]) for p in range(2)
        )
    keys = 4 * width
    held[:, keys:] = two_terms(squares)
    half, few = held.shape[0] // 2, held.shape[0] // 8
    rounds = matching.shape[0]
    column = lax.broadcasted_iota(jnp.int32, matching.shape, 1) == h
    owner = jnp.sum(jnp.where(column, matching[...], 0), axis=1, keepdims=True)
    lane = lax.broadcasted_iota(jnp.int32, (2 * few, 128), 1)
    for k, out in enumerate(outs):
        start = pl.multiple_of((h ^ k) * few, 8)
        part = jnp.concatenate(
            [held[pl.ds(start, few), :], held[pl.ds(half + start, few), :]], axis=0
        )
        live = sum(
            jnp.where(owner[r : r + 1] == (h ^ k), counts[:, r : r + 1], 0) for r in range(rounds)
        )
        out[:, :keys] = part[:, :keys].astype(out.dtype)
        tail = jnp.where(lane == 32, live.astype(jnp.float32), part[:, keys:])
        out[:, keys:] = tail.astype(out.dtype)


def group_kernel(places, *refs):
    parts, kept, sent, live = refs[:4], refs[4], refs[5], refs[6]
    h = lax.axis_index("hold")
    keys = kept.shape[1] - 128
    total = sum(part[...].astype(jnp.float32) for part in parts)
    for k, part in zip((*places, 0), parts, strict=True):
        live[pl.ds(h ^ k, 1), :] = part[:1, keys:].astype(jnp.float32)
    squares = two_terms(total[:, keys : keys + 1] + total[:, -1:])
    rows = kept.shape[0]
    kept[:, :keys] = total[:rows, :keys]
    kept[:, keys:] = squares[:rows]
    sent[:, :keys] = total[rows:, :keys].astype(jnp.bfloat16)
    sent[:, keys:] = squares[rows:].astype(jnp.bfloat16)


def last_kernel(width, kept, came, matching, live, out):
    h = lax.axis_index("hold")
    _, rounds, block, features = out.shape
    total = kept[...] + came[...].astype(jnp.float32)
    squares = total[:, features : features + 1] + total[:, -1:]
    keys = total[:, :features] * lax.rsqrt(squares / width + EPSILON)
    b_of = lax.broadcasted_iota(jnp.int32, (block, 1), 0).astype(jnp.float32)
    blocks = []
    for i in range(rounds):
        part = keys[i * block : (i + 1) * block]
        blocks.append(jnp.where(b_of < live[i : i + 1, 32:33], part, 0.0))
    for r in range(rounds):
        picked = sum(
            jnp.where(matching[r : r + 1, i : i + 1] == h, blocks[i], 0.0) for i in range(rounds)
        )
        out[0, r] = picked.astype(jnp.bfloat16)


def rows_past_weights(cache, ln_gain, w_fc1, w_fc2, norm_gain, w_key, matching, counts, width):
    n = lax.axis_size("hold")
    rounds, block, depth = cache.shape[1:]
    rows = rounds * block
    chunk = depth // n
    hidden_cols, out_cols, key_cols = w_fc1.shape[1], w_fc2.shape[1], w_key.shape[1]
    share = w_key.shape[0] // n
    f32, bf16 = jnp.float32, jnp.bfloat16
    vmem = pltpu.VMEM

    def like(dims, kind=bf16):
        return jax.ShapeDtypeStruct(dims, kind)

    long = 8 << 30
    hbm = pl.BlockSpec(memory_space=pltpu.HBM)
    in_hbm = [
        pltpu.with_memory_space_constraint(x, pltpu.HBM)
        for x in (cache, ln_gain, matching, w_fc1, w_fc2, w_key)
    ]
    cache_other = swap(cache, "tp", 2, 1)
    own, w_fc1_mine, w_fc2_mine, key_0, key_1, key_far = call(
        own_kernel,
        [like((rows, depth), f32), like(w_fc1.shape), like(w_fc2.shape)]
        + [like((share, key_cols))] * 3,
        *in_hbm,
        in_specs=[hbm] * 6,
        scratch=[
            vmem(cache.shape, bf16),
            vmem(ln_gain.shape, f32),
            vmem(matching.shape, jnp.int32),
            pltpu.SemaphoreType.DMA((8,)),
        ],
        flops=long,
    )
    w_fc1_other = swap(w_fc1, "rep", 2, 1)
    gain_other = swap(norm_gain, "rep", 2, 1)
    own, cache_other, w_fc2_sent, w_fc1_other, gain_other = lax.optimization_barrier(
        (own, cache_other, w_fc2_mine, w_fc1_other, gain_other)
    )
    w_fc2_other = swap(w_fc2_sent, "rep", 2, 1)
    pieces = call(
        both_kernel,
        [like((2 * rows, chunk))] * n,
        own,
        cache_other,
        ln_gain,
        matching,
        scratch=[vmem((rows, depth), f32)],
    )

    *pieces, key_1, key_far = lax.optimization_barrier((*pieces, key_1, key_far))
    key_1 = swap(key_1, "hold", n, 1)
    perm = [(n * g + a, n * g + (a ^ 3 ^ g)) for g in range(2) for a in range(n)]
    key_far = lax.ppermute(key_far, ("grp", "hold"), perm)

    order = (3, 2, 1)
    partial = call(
        functools.partial(first_kernel, order),
        [like((4 * rows, hidden_cols))] * n,
        *exchange(pieces, order),
        w_fc1_mine,
        w_fc1_other,
        scratch=[vmem((8 * rows, chunk), f32), vmem((2, 8 * rows, hidden_cols), f32)],
        flops=long,
    )
    *partial, w_fc2_other = lax.optimization_barrier((*partial, w_fc2_other))
    key_near = swap(key_far, "grp", 2, 1)
    parts = exchange(partial, (1, 3, 2))
    hidden = call(gelu_kernel, like(parts[0].shape), *parts, flops=long)
    hidden, key_far = lax.optimization_barrier((hidden, key_far))

    halves = []
    for g in range(2):
        perm = [
            (2 * a + b, 2 * (2 * b + (a >> 1)) + ((a & 1) ^ (a >> 1) ^ b ^ g))
            for a in range(n)
            for b in range(2)
        ]
        halves.append(lax.ppermute(hidden, ("hold", "tp"), perm))
    *halves, key_1 = lax.optimization_barrier((*halves, key_1))
    merged = call(
        second_kernel,
        [like((8 * rows, 2 * share))] * n,
        *halves,
        w_fc2_mine,
        w_fc2_other,
        scratch=[vmem((2, 8 * rows, out_cols), f32)],
        flops=32 * rows * w_fc2.size,
    )
    *merged, key_near = lax.optimization_barrier((*merged, key_near))
    key_mine = jnp.concatenate([key_0, key_1, key_far, key_near])
    key_other = swap(key_mine, "rep", 2, 1)
    wide = n * key_cols + 128
    keys = call(
        key_kernel,
        [like((2 * rows, wide), f32)] + [like((2 * rows, wide))] * (n - 1),
        *exchange(merged, (2, 1, 3)),
        key_mine,
        key_other,
        norm_gain,
        gain_other,
        matching,
        counts.reshape(1, rounds),
        scratch=[vmem((8 * rows, wide), f32)],
        flops=32 * rows * w_key.size,
    )
    order = (3, 2, 1)
    kept, sent, live = call(
        functools.partial(group_kernel, order),
        [like((rows, wide), f32), like((rows, wide)), like((n, 128), f32)],
        *exchange(keys, order),
    )
    return call(
        functools.partial(last_kernel, width),
        like((1, rounds, block, n * key_cols)),
        kept,
        swap(sent, "tp", 2, 1),
        matching,
        live,
    )


def per_device(cache, ln_gain, w_fc1, w_fc2, norm_gain, w_key, matching, counts):
    sizes = lax.axis_size("hold"), lax.axis_size("tp"), lax.axis_size("rep")
    rounds, block, depth = cache.shape[1:]
    group = sizes[1] * sizes[2]
    width = w_key.shape[0] * group
    few = sizes[0] * rounds * group * block <= w_fc1.shape[1]
    fits = sizes == (4, 2, 2) and rounds == 4 and block == 2
    plan = rows_past_weights if few and fits else rows_to_owners
    return plan(cache, ln_gain, w_fc1, w_fc2, norm_gain, w_key, matching, counts, width)


def solution(mesh):
    return jax.shard_map(
        per_device,
        mesh=mesh,
        in_specs=(
            P(("grp", "hold"), None, ("tp", "rep"), None),
            P(),
            P("hold", ("tp", "rep")),
            P("hold", ("tp", "rep")),
            P(("tp", "rep")),
            P(("tp", "rep"), "hold"),
            P("grp", None),
            P(("grp", "hold"), None, ("tp", "rep")),
        ),
        out_specs=P(("grp", "hold"), None, ("tp", "rep"), None),
        check_vma=False,
    )
```

```python
import functools

import jax
import jax.numpy as jnp
from jax import lax
from jax.experimental import pallas as pl
from jax.experimental.pallas import tpu as pltpu
from jax.sharding import PartitionSpec as P

EPSILON = 1e-06
GROUP_AXES = ("tp", "rep")
ALL_AXES = ("hold", "tp", "rep")


def patch_norm(rows, ln_gain):
    width = ln_gain.shape[0]
    patches = rows.astype(jnp.float32).reshape(rows.shape[0], -1, width)
    scale = lax.rsqrt(jnp.mean(patches * patches, axis=2, keepdims=True) + EPSILON)
    return patches * scale * ln_gain


def merger_features(rows, ln_gain, w_fc1, w_fc2, norm_gain, width):
    normed = patch_norm(rows, ln_gain).reshape(rows.shape[0], -1).astype(jnp.bfloat16)
    first_cols = lax.all_gather(w_fc1, "hold", axis=0, tiled=True)
    product = jnp.dot(
        lax.all_gather(normed, GROUP_AXES, axis=0, tiled=True),
        first_cols,
        preferred_element_type=jnp.float32,
    )
    hidden = jax.nn.gelu(product, approximate=False).astype(jnp.bfloat16)
    second_cols = lax.all_gather(w_fc2, "hold", axis=0, tiled=True)
    merged = jnp.dot(
        lax.all_gather(hidden, GROUP_AXES, axis=1, tiled=True),
        second_cols,
        preferred_element_type=jnp.float32,
    )
    squares = lax.psum(jnp.sum(merged * merged, axis=1), GROUP_AXES)
    scale = lax.rsqrt(squares / width + EPSILON)
    return (merged * scale[:, None] * norm_gain).astype(jnp.bfloat16)


def rows_to_owners(cache, ln_gain, w_fc1, w_fc2, norm_gain, w_key, matching, counts, width):
    rounds = cache.shape[1]
    block = cache.shape[2]
    holder_index = lax.axis_index("hold")
    owner_column = lax.dynamic_slice_in_dim(matching, holder_index, 1, 1)[:, 0]
    send_order = jnp.argsort(owner_column)
    source_of = jnp.argmax(matching == holder_index, axis=1)
    sent_counts = jnp.take(counts[0, :, 0], send_order)
    outgoing = jnp.take(cache[0], send_order, axis=0)
    arrived = lax.all_to_all(outgoing, "hold", split_axis=0, concat_axis=0, tiled=True)
    arrived_counts = lax.all_to_all(
        sent_counts.reshape(rounds, 1), "hold", split_axis=0, concat_axis=0, tiled=True
    )
    own_blocks = jnp.take(arrived, source_of, axis=0)
    own_counts = jnp.take(arrived_counts[:, 0], source_of)
    features = merger_features(
        own_blocks.reshape(rounds * block, -1), ln_gain, w_fc1, w_fc2, norm_gain, width
    )
    key_cols = lax.all_gather(w_key, "hold", axis=1, tiled=True)
    keys = lax.psum_scatter(
        jnp.dot(features, key_cols, preferred_element_type=jnp.float32),
        GROUP_AXES,
        scatter_dimension=0,
        tiled=True,
    )
    keys = keys.reshape(rounds, block, -1)
    valid = jnp.arange(block, dtype=jnp.int32)[None, :] < own_counts[:, None]
    keys = jnp.where(valid[:, :, None], keys, jnp.zeros_like(keys))
    return keys.astype(jnp.bfloat16)[None]


def swap(x, axis, n, step):
    return lax.ppermute(x, axis, [(i, i ^ step) for i in range(n)])


def exchange(parts, order):
    n = len(parts)
    return [swap(parts[k], "hold", n, k) for k in order] + [parts[0]]


def call(body, outs, *args, flops=0, scratch=(), **specs):
    moved = sum(x.size * x.dtype.itemsize for x in args)
    return pl.pallas_call(
        body,
        out_shape=outs,
        scratch_shapes=scratch,
        cost_estimate=pl.CostEstimate(flops=flops, bytes_accessed=moved, transcendentals=0),
        compiler_params=pltpu.CompilerParams(vmem_limit_bytes=16 << 20),
        **specs,
    )(*args)


def dot(a, b):
    return jnp.dot(a, b, preferred_element_type=jnp.float32)


def norm_rows(cache, gain, matching, held):
    h = lax.axis_index("hold")
    _, rounds, block, depth = cache.shape
    width = gain.shape[1]
    column = lax.broadcasted_iota(jnp.int32, matching.shape, 1) == h
    owner = jnp.sum(jnp.where(column, matching[...], 0), axis=1, keepdims=True)
    for p in range(depth // width):
        cols = pl.ds(p * width, width)
        normed = []
        for r in range(rounds):
            x = cache[0, r, :, cols].astype(jnp.float32)
            scale = lax.rsqrt(jnp.mean(x * x, axis=1, keepdims=True) + EPSILON)
            normed.append(x * scale * gain)
        for j in range(rounds):
            picked = sum(
                jnp.where(owner[r : r + 1] == j, normed[r], 0.0) for r in range(rounds)
            )
            held[j * block : (j + 1) * block, cols] = picked


def own_kernel(cache, ln_gain, matching, w_fc1, w_fc2, w_key, *refs):
    out, held_1, held_2, *key_rows = refs[:6]
    x_in, gain_in, plan_in, sems = refs[6:]
    h, grp = lax.axis_index("hold"), lax.axis_index("grp")
    pairs = [(cache, x_in), (ln_gain, gain_in), (matching, plan_in), (w_fc1, held_1), (w_fc2, held_2)]
    share = key_rows[0].shape[0]
    for place, end in zip((h, h ^ 1, h ^ 3 ^ grp), key_rows, strict=True):
        pairs.append((w_key.at[pl.ds(pl.multiple_of(place * share, 128), share)], end))
    copies = [pltpu.make_async_copy(a, b, sems.at[i]) for i, (a, b) in enumerate(pairs)]
    for copy in copies:
        copy.start()
    for copy in copies[:3]:
        copy.wait()
    norm_rows(x_in, gain_in[...].reshape(1, -1), plan_in, out)
    for copy in copies[3:]:
        copy.wait()


def both_kernel(own, cache, ln_gain, matching, *refs):
    outs, held = refs[:4], refs[4]
    h = lax.axis_index("hold")
    norm_rows(cache, ln_gain[...].reshape(1, -1), matching, held)
    chunk = outs[0].shape[1]
    for s, out in enumerate(outs):
        cols = pl.ds(pl.multiple_of((h ^ s) * chunk, 128), chunk)
        out[...] = jnp.concatenate([own[:, cols], held[:, cols]], axis=0).astype(jnp.bfloat16)


def first_kernel(places, *refs):
    pieces, weights, outs = refs[:4], refs[4:6], refs[6:10]
    rows, sums = refs[10:]
    h, rep = lax.axis_index("hold"), lax.axis_index("rep")
    size = pieces[0].shape[0] // 2
    half = 4 * size
    for k, piece in zip((*places, 0), pieces, strict=True):
        part = piece[...].astype(jnp.float32)
        for b in range(2):
            start = pl.multiple_of(b * half + (h ^ k) * size, 8)
            rows[pl.ds(start, size), :] = part[b * size : (b + 1) * size]
    x = rows[...].astype(jnp.bfloat16)
    for i, weight in enumerate(weights):
        sums[rep ^ i] = dot(x, weight[...])
    for k, out in enumerate(outs):
        start = pl.multiple_of(((h ^ k) & 1) * half, 16)
        out[...] = sums[(h ^ k) >> 1, pl.ds(start, half), :].astype(jnp.bfloat16)


ERFC_NEAR = (
    2.326819970068386e-2,
    -1.387039388740657e-1,
    3.687424674597105e-1,
    -5.824733027278666e-1,
    6.210004621745983e-1,
    -4.944515323274145e-1,
    3.404879937665872e-1,
    -2.741127028184656e-1,
    5.638259427386472e-1,
)
ERFC_FAR = (
    -1.047766399936249e1,
    1.297719955372516e1,
    -7.495518717768503e0,
    2.921019019210786e0,
    -1.015265279202700e0,
    4.218463358204948e-1,
    -2.820767439740514e-1,
    5.641895067754075e-1,
)


def erfc(x):
    size = jnp.maximum(jnp.abs(x), 1.0)
    inverse = 1.0 / size
    square = inverse * inverse
    near, far = jnp.zeros_like(x), jnp.zeros_like(x)
    for c in ERFC_NEAR:
        near = near * square + c
    for c in ERFC_FAR:
        far = far * square + c
    tail = jnp.exp(-size * size) * inverse * jnp.where(size < 2.0, near, far)
    return jnp.where(jnp.abs(x) < 1.0, 1.0 - lax.erf(x), jnp.where(x < 0, 2.0 - tail, tail))


def gelu_kernel(*refs):
    x = sum(part[...].astype(jnp.float32) for part in refs[:4])
    refs[4][...] = (0.5 * x * erfc(-x * 0.5**0.5)).astype(jnp.bfloat16)


def second_kernel(first, second, w_mine, w_other, *refs):
    outs, sums = refs[:4], refs[4]
    h = lax.axis_index("hold")
    half = first.shape[0]
    bb = half // 16
    to = lax.broadcasted_iota(jnp.int32, (2 * half, half), 0)
    source = lax.broadcasted_iota(jnp.int32, (2 * half, half), 1)
    u, owner = to // half, (to % half) // (4 * bb)
    holder, b_of = (to % (4 * bb)) // bb, to % bb
    wanted = (u ^ (h & 1)) * half + (holder * 4 + owner) * bb + b_of
    moved = 0.0
    for p, part in enumerate((first, second)):
        order = jnp.where(source + p * half == wanted, 1.0, 0.0)
        moved += dot(order.astype(jnp.bfloat16), part[...])
    moved = moved.astype(jnp.bfloat16)
    cols = outs[0].shape[1] // 2
    for p, weight in enumerate((w_mine, w_other)):
        sums[p] = dot(moved, weight[...])
        for k in range(4):
            start = pl.multiple_of((h ^ k) * cols, 128)
            part = sums[p, :, pl.ds(start, cols)].astype(jnp.bfloat16)
            outs[k][:, p * cols : (p + 1) * cols] = part


def two_terms(x):
    high = x.astype(jnp.bfloat16).astype(jnp.float32)
    lane = lax.broadcasted_iota(jnp.int32, (x.shape[0], 128), 1)
    return jnp.where(lane < 64, high, x - high)


def key_kernel(*refs):
    parts, blocks, gains, matching, counts = refs[:4], refs[4:6], refs[6:8], refs[8], refs[9]
    outs, held = refs[10:14], refs[14]
    h, grp = lax.axis_index("hold"), lax.axis_index("grp")
    merged = sum(part[...].astype(jnp.float32) for part in parts)
    squares = jnp.sum(merged * merged, axis=1, keepdims=True)
    cols = merged.shape[1] // 2
    start = pl.multiple_of(h * cols, 128)
    rows = []
    for p in range(2):
        gain = gains[p][pl.ds(start, cols)].reshape(1, cols)
        rows.append((merged[:, p * cols : (p + 1) * cols] * gain).astype(jnp.bfloat16))
    width = blocks[0].shape[1]
    for i, place in enumerate((h, h ^ 1, h ^ 3 ^ grp, h ^ 2 ^ grp)):
        held[:, pl.ds(pl.multiple_of(place * width, 128), width)] = sum(
            dot(rows[p], blocks[p][i * cols : (i + 1) * cols, :]) for p in range(2)
        )
    keys = 4 * width
    held[:, keys:] = two_terms(squares)
    half, few = held.shape[0] // 2, held.shape[0] // 8
    rounds = matching.shape[0]
    column = lax.broadcasted_iota(jnp.int32, matching.shape, 1) == h
    owner = jnp.sum(jnp.where(column, matching[...], 0), axis=1, keepdims=True)
    lane = lax.broadcasted_iota(jnp.int32, (2 * few, 128), 1)
    for k, out in enumerate(outs):
        start = pl.multiple_of((h ^ k) * few, 8)
        part = jnp.concatenate(
            [held[pl.ds(start, few), :], held[pl.ds(half + start, few), :]], axis=0
        )
        live = sum(
            jnp.where(owner[r : r + 1] == (h ^ k), counts[:, r : r + 1], 0) for r in range(rounds)
        )
        out[:, :keys] = part[:, :keys].astype(out.dtype)
        tail = jnp.where(lane == 32, live.astype(jnp.float32), part[:, keys:])
        out[:, keys:] = tail.astype(out.dtype)


def group_kernel(places, *refs):
    parts, kept, sent, live = refs[:4], refs[4], refs[5], refs[6]
    h = lax.axis_index("hold")
    keys = kept.shape[1] - 128
    total = sum(part[...].astype(jnp.float32) for part in parts)
    for k, part in zip((*places, 0), parts, strict=True):
        live[pl.ds(h ^ k, 1), :] = part[:, keys:].astype(jnp.float32)[:1]
    squares = two_terms(total[:, keys : keys + 1] + total[:, -1:])
    rows = kept.shape[0]
    kept[:, :keys] = total[:rows, :keys]
    kept[:, keys:] = squares[:rows]
    sent[:, :keys] = total[rows:, :keys].astype(jnp.bfloat16)
    sent[:, keys:] = squares[rows:].astype(jnp.bfloat16)


def last_kernel(width, kept, came, matching, live, out):
    h = lax.axis_index("hold")
    _, rounds, block, features = out.shape
    total = kept[...] + came[...].astype(jnp.float32)
    squares = total[:, features : features + 1] + total[:, -1:]
    keys = total[:, :features] * lax.rsqrt(squares / width + EPSILON)
    b_of = lax.broadcasted_iota(jnp.int32, (block, 1), 0).astype(jnp.float32)
    blocks = []
    for i in range(rounds):
        part = keys[i * block : (i + 1) * block]
        blocks.append(jnp.where(b_of < live[i : i + 1, 32:33], part, 0.0))
    for r in range(rounds):
        picked = sum(
            jnp.where(matching[r : r + 1, i : i + 1] == h, blocks[i], 0.0) for i in range(rounds)
        )
        out[0, r] = picked.astype(jnp.bfloat16)


def rows_past_weights(cache, ln_gain, w_fc1, w_fc2, norm_gain, w_key, matching, counts, width):
    n = lax.axis_size("hold")
    rounds, block, depth = cache.shape[1:]
    rows = rounds * block
    chunk = depth // n
    hidden_cols, out_cols, key_cols = w_fc1.shape[1], w_fc2.shape[1], w_key.shape[1]
    share = w_key.shape[0] // n
    f32, bf16 = jnp.float32, jnp.bfloat16
    vmem = pltpu.VMEM

    def like(dims, kind=bf16):
        return jax.ShapeDtypeStruct(dims, kind)

    long = 8 << 30
    hbm = pl.BlockSpec(memory_space=pltpu.HBM)
    in_hbm = [
        pltpu.with_memory_space_constraint(x, pltpu.HBM)
        for x in (cache, ln_gain, matching, w_fc1, w_fc2, w_key)
    ]
    cache_other = swap(cache, "tp", 2, 1)
    own, w_fc1_mine, w_fc2_mine, key_0, key_1, key_far = call(
        own_kernel,
        [like((rows, depth), f32), like(w_fc1.shape), like(w_fc2.shape)]
        + [like((share, key_cols))] * 3,
        *in_hbm,
        in_specs=[hbm] * 6,
        scratch=[
            vmem(cache.shape, bf16),
            vmem(ln_gain.shape, f32),
            vmem(matching.shape, jnp.int32),
            pltpu.SemaphoreType.DMA((8,)),
        ],
        flops=long,
    )
    w_fc1_other = swap(w_fc1, "rep", 2, 1)
    gain_other = swap(norm_gain, "rep", 2, 1)
    own, cache_other, w_fc2_sent, w_fc1_other, gain_other = lax.optimization_barrier(
        (own, cache_other, w_fc2_mine, w_fc1_other, gain_other)
    )
    w_fc2_other = swap(w_fc2_sent, "rep", 2, 1)
    pieces = call(
        both_kernel,
        [like((2 * rows, chunk))] * n,
        own,
        cache_other,
        ln_gain,
        matching,
        scratch=[vmem((rows, depth), f32)],
    )

    *pieces, key_1, key_far = lax.optimization_barrier((*pieces, key_1, key_far))
    key_1 = swap(key_1, "hold", n, 1)
    perm = [(n * g + a, n * g + (a ^ 3 ^ g)) for g in range(2) for a in range(n)]
    key_far = lax.ppermute(key_far, ("grp", "hold"), perm)

    order = (3, 2, 1)
    partial = call(
        functools.partial(first_kernel, order),
        [like((4 * rows, hidden_cols))] * n,
        *exchange(pieces, order),
        w_fc1_mine,
        w_fc1_other,
        scratch=[vmem((8 * rows, chunk), f32), vmem((2, 8 * rows, hidden_cols), f32)],
        flops=long,
    )
    *partial, w_fc2_other = lax.optimization_barrier((*partial, w_fc2_other))
    key_near = swap(key_far, "grp", 2, 1)
    parts = exchange(partial, (1, 3, 2))
    hidden = call(gelu_kernel, like(parts[0].shape), *parts, flops=long)
    hidden, key_far = lax.optimization_barrier((hidden, key_far))

    halves = []
    for g in range(2):
        perm = [
            (2 * a + b, 2 * (2 * b + (a >> 1)) + ((a & 1) ^ (a >> 1) ^ b ^ g))
            for a in range(n)
            for b in range(2)
        ]
        halves.append(lax.ppermute(hidden, ("hold", "tp"), perm))
    *halves, key_1 = lax.optimization_barrier((*halves, key_1))
    merged = call(
        second_kernel,
        [like((8 * rows, 2 * share))] * n,
        *halves,
        w_fc2_mine,
        w_fc2_other,
        scratch=[vmem((2, 8 * rows, out_cols), f32)],
        flops=32 * rows * w_fc2.size,
    )
    *merged, key_near = lax.optimization_barrier((*merged, key_near))
    key_mine = jnp.concatenate([key_0, key_1, key_far, key_near])
    key_other = swap(key_mine, "rep", 2, 1)
    wide = n * key_cols + 128
    keys = call(
        key_kernel,
        [like((2 * rows, wide), f32)] + [like((2 * rows, wide))] * (n - 1),
        *exchange(merged, (2, 1, 3)),
        key_mine,
        key_other,
        norm_gain,
        gain_other,
        matching,
        counts.reshape(1, rounds),
        scratch=[vmem((8 * rows, wide), f32)],
        flops=32 * rows * w_key.size,
    )
    order = (3, 2, 1)
    kept, sent, live = call(
        functools.partial(group_kernel, order),
        [like((rows, wide), f32), like((rows, wide)), like((n, 128), f32)],
        *exchange(keys, order),
    )
    return call(
        functools.partial(last_kernel, width),
        like((1, rounds, block, n * key_cols)),
        kept,
        swap(sent, "tp", 2, 1),
        matching,
        live,
    )


def per_device(cache, ln_gain, w_fc1, w_fc2, norm_gain, w_key, matching, counts):
    sizes = lax.axis_size("hold"), lax.axis_size("tp"), lax.axis_size("rep")
    rounds, block, depth = cache.shape[1:]
    group = sizes[1] * sizes[2]
    width = w_key.shape[0] * group
    few = sizes[0] * rounds * group * block <= w_fc1.shape[1]
    fits = sizes == (4, 2, 2) and rounds == 4 and block == 2
    plan = rows_past_weights if few and fits else rows_to_owners
    return plan(cache, ln_gain, w_fc1, w_fc2, norm_gain, w_key, matching, counts, width)


def solution(mesh):
    return jax.shard_map(
        per_device,
        mesh=mesh,
        in_specs=(
            P(("grp", "hold"), None, ("tp", "rep"), None),
            P(),
            P("hold", ("tp", "rep")),
            P("hold", ("tp", "rep")),
            P(("tp", "rep")),
            P(("tp", "rep"), "hold"),
            P("grp", None),
            P(("grp", "hold"), None, ("tp", "rep")),
        ),
        out_specs=P(("grp", "hold"), None, ("tp", "rep"), None),
        check_vma=False,
    )
```

```python
import functools

import jax
import jax.numpy as jnp
from jax import lax
from jax.experimental import pallas as pl
from jax.experimental.pallas import tpu as pltpu
from jax.sharding import PartitionSpec as P

EPSILON = 1e-06
GROUP_AXES = ("tp", "rep")
ALL_AXES = ("hold", "tp", "rep")


def patch_norm(rows, ln_gain):
    width = ln_gain.shape[0]
    patches = rows.astype(jnp.float32).reshape(rows.shape[0], -1, width)
    scale = lax.rsqrt(jnp.mean(patches * patches, axis=2, keepdims=True) + EPSILON)
    return patches * scale * ln_gain


def merger_features(rows, ln_gain, w_fc1, w_fc2, norm_gain, width):
    normed = patch_norm(rows, ln_gain).reshape(rows.shape[0], -1).astype(jnp.bfloat16)
    first_cols = lax.all_gather(w_fc1, "hold", axis=0, tiled=True)
    product = jnp.dot(
        lax.all_gather(normed, GROUP_AXES, axis=0, tiled=True),
        first_cols,
        preferred_element_type=jnp.float32,
    )
    hidden = jax.nn.gelu(product, approximate=False).astype(jnp.bfloat16)
    second_cols = lax.all_gather(w_fc2, "hold", axis=0, tiled=True)
    merged = jnp.dot(
        lax.all_gather(hidden, GROUP_AXES, axis=1, tiled=True),
        second_cols,
        preferred_element_type=jnp.float32,
    )
    squares = lax.psum(jnp.sum(merged * merged, axis=1), GROUP_AXES)
    scale = lax.rsqrt(squares / width + EPSILON)
    return (merged * scale[:, None] * norm_gain).astype(jnp.bfloat16)


def rows_to_owners(cache, ln_gain, w_fc1, w_fc2, norm_gain, w_key, matching, counts, width):
    rounds = cache.shape[1]
    block = cache.shape[2]
    holder_index = lax.axis_index("hold")
    owner_column = lax.dynamic_slice_in_dim(matching, holder_index, 1, 1)[:, 0]
    send_order = jnp.argsort(owner_column)
    source_of = jnp.argmax(matching == holder_index, axis=1)
    sent_counts = jnp.take(counts[0, :, 0], send_order)
    outgoing = jnp.take(cache[0], send_order, axis=0)
    arrived = lax.all_to_all(outgoing, "hold", split_axis=0, concat_axis=0, tiled=True)
    arrived_counts = lax.all_to_all(
        sent_counts.reshape(rounds, 1), "hold", split_axis=0, concat_axis=0, tiled=True
    )
    own_blocks = jnp.take(arrived, source_of, axis=0)
    own_counts = jnp.take(arrived_counts[:, 0], source_of)
    features = merger_features(
        own_blocks.reshape(rounds * block, -1), ln_gain, w_fc1, w_fc2, norm_gain, width
    )
    key_cols = lax.all_gather(w_key, "hold", axis=1, tiled=True)
    keys = lax.psum_scatter(
        jnp.dot(features, key_cols, preferred_element_type=jnp.float32),
        GROUP_AXES,
        scatter_dimension=0,
        tiled=True,
    )
    keys = keys.reshape(rounds, block, -1)
    valid = jnp.arange(block, dtype=jnp.int32)[None, :] < own_counts[:, None]
    keys = jnp.where(valid[:, :, None], keys, jnp.zeros_like(keys))
    return keys.astype(jnp.bfloat16)[None]


def swap(x, axis, n, step):
    return lax.ppermute(x, axis, [(i, i ^ step) for i in range(n)])


def exchange(parts, order):
    n = len(parts)
    return [swap(parts[k], "hold", n, k) for k in order] + [parts[0]]


def call(body, outs, *args, flops=0, scratch=(), **specs):
    moved = sum(x.size * x.dtype.itemsize for x in args)
    return pl.pallas_call(
        body,
        out_shape=outs,
        scratch_shapes=scratch,
        cost_estimate=pl.CostEstimate(flops=flops, bytes_accessed=moved, transcendentals=0),
        compiler_params=pltpu.CompilerParams(vmem_limit_bytes=16 << 20),
        **specs,
    )(*args)


def dot(a, b):
    return jnp.dot(a, b, preferred_element_type=jnp.float32)


def norm_rows(cache, gain, matching, held):
    h = lax.axis_index("hold")
    _, rounds, block, depth = cache.shape
    width = gain.shape[1]
    column = lax.broadcasted_iota(jnp.int32, matching.shape, 1) == h
    owner = jnp.sum(jnp.where(column, matching[...], 0), axis=1, keepdims=True)
    for p in range(depth // width):
        cols = pl.ds(p * width, width)
        normed = []
        for r in range(rounds):
            x = cache[0, r, :, cols].astype(jnp.float32)
            scale = lax.rsqrt(jnp.mean(x * x, axis=1, keepdims=True) + EPSILON)
            normed.append(x * scale * gain)
        for j in range(rounds):
            picked = sum(
                jnp.where(owner[r : r + 1] == j, normed[r], 0.0) for r in range(rounds)
            )
            held[j * block : (j + 1) * block, cols] = picked


def own_kernel(cache, ln_gain, matching, w_fc1, w_fc2, w_key, *refs):
    out, held_1, held_2, *key_rows = refs[:6]
    x_in, gain_in, plan_in, sems = refs[6:]
    h, grp = lax.axis_index("hold"), lax.axis_index("grp")
    pairs = [(cache, x_in), (ln_gain, gain_in), (matching, plan_in), (w_fc1, held_1), (w_fc2, held_2)]
    share = key_rows[0].shape[0]
    for place, end in zip((h, h ^ 1, h ^ 3 ^ grp), key_rows, strict=True):
        pairs.append((w_key.at[pl.ds(pl.multiple_of(place * share, 128), share)], end))
    copies = [pltpu.make_async_copy(a, b, sems.at[i]) for i, (a, b) in enumerate(pairs)]
    for copy in copies:
        copy.start()
    for copy in copies[:3]:
        copy.wait()
    norm_rows(x_in, gain_in[...].reshape(1, -1), plan_in, out)
    for copy in copies[3:]:
        copy.wait()


def both_kernel(own, cache, ln_gain, matching, *refs):
    outs, held = refs[:4], refs[4]
    h = lax.axis_index("hold")
    norm_rows(cache, ln_gain[...].reshape(1, -1), matching, held)
    chunk = outs[0].shape[1]
    for s, out in enumerate(outs):
        cols = pl.ds(pl.multiple_of((h ^ s) * chunk, 128), chunk)
        out[...] = jnp.concatenate([own[:, cols], held[:, cols]], axis=0).astype(jnp.bfloat16)


def first_kernel(places, *refs):
    pieces, weights, outs = refs[:4], refs[4:6], refs[6:10]
    rows, sums = refs[10:]
    h, rep = lax.axis_index("hold"), lax.axis_index("rep")
    size = pieces[0].shape[0] // 2
    half = 4 * size
    for k, piece in zip((*places, 0), pieces, strict=True):
        part = piece[...].astype(jnp.float32)
        for b in range(2):
            start = pl.multiple_of(b * half + (h ^ k) * size, 8)
            rows[pl.ds(start, size), :] = part[b * size : (b + 1) * size]
    x = rows[...].astype(jnp.bfloat16)
    for i, weight in enumerate(weights):
        sums[rep ^ i] = dot(x, weight[...])
    for k, out in enumerate(outs):
        start = pl.multiple_of(((h ^ k) & 1) * half, 16)
        out[...] = sums[(h ^ k) >> 1, pl.ds(start, half), :].astype(jnp.bfloat16)


ERFC_NEAR = (
    2.326819970068386e-2,
    -1.387039388740657e-1,
    3.687424674597105e-1,
    -5.824733027278666e-1,
    6.210004621745983e-1,
    -4.944515323274145e-1,
    3.404879937665872e-1,
    -2.741127028184656e-1,
    5.638259427386472e-1,
)
ERFC_FAR = (
    -1.047766399936249e1,
    1.297719955372516e1,
    -7.495518717768503e0,
    2.921019019210786e0,
    -1.015265279202700e0,
    4.218463358204948e-1,
    -2.820767439740514e-1,
    5.641895067754075e-1,
)


def erfc(x):
    size = jnp.maximum(jnp.abs(x), 1.0)
    inverse = 1.0 / size
    square = inverse * inverse
    near, far = jnp.zeros_like(x), jnp.zeros_like(x)
    for c in ERFC_NEAR:
        near = near * square + c
    for c in ERFC_FAR:
        far = far * square + c
    tail = jnp.exp(-size * size) * inverse * jnp.where(size < 2.0, near, far)
    return jnp.where(jnp.abs(x) < 1.0, 1.0 - lax.erf(x), jnp.where(x < 0, 2.0 - tail, tail))


def gelu_kernel(*refs):
    x = sum(part[...].astype(jnp.float32) for part in refs[:4])
    hidden = (0.5 * x * erfc(-x * 0.5**0.5)).astype(jnp.bfloat16)
    total = x.shape[0]
    bb = total // 16
    to = lax.broadcasted_iota(jnp.int32, (total, total), 0)
    source = lax.broadcasted_iota(jnp.int32, (total, total), 1)
    owner, holder = to // (4 * bb), (to % (4 * bb)) // bb
    order = jnp.where(source == (holder * 4 + owner) * bb + to % bb, 1.0, 0.0)
    refs[4][...] = dot(order.astype(jnp.bfloat16), hidden).astype(jnp.bfloat16)


def second_kernel(first, second, w_mine, w_other, *refs):
    outs, rows = refs[:4], refs[4]
    h = lax.axis_index("hold")
    half = first.shape[0]
    for g, part in enumerate((first, second)):
        rows[pl.ds(pl.multiple_of((g ^ (h & 1)) * half, 16), half), :] = part[...]
    x = rows[...]
    cols = outs[0].shape[1] // 2
    for p, weight in enumerate((w_mine, w_other)):
        for k, out in enumerate(outs):
            start = pl.multiple_of((h ^ k) * cols, 128)
            part = dot(x, weight[:, pl.ds(start, cols)]).astype(jnp.bfloat16)
            out[:, p * cols : (p + 1) * cols] = part


def two_terms(x):
    high = x.astype(jnp.bfloat16).astype(jnp.float32)
    lane = lax.broadcasted_iota(jnp.int32, (x.shape[0], 128), 1)
    return jnp.where(lane < 64, high, x - high)


def key_kernel(*refs):
    parts, blocks, gains, matching, counts = refs[:4], refs[4:6], refs[6:8], refs[8], refs[9]
    outs, held = refs[10:14], refs[14]
    h, grp = lax.axis_index("hold"), lax.axis_index("grp")
    merged = sum(part[...].astype(jnp.float32) for part in parts)
    squares = jnp.sum(merged * merged, axis=1, keepdims=True)
    cols = merged.shape[1] // 2
    start = pl.multiple_of(h * cols, 128)
    rows = []
    for p in range(2):
        gain = gains[p][pl.ds(start, cols)].reshape(1, cols)
        rows.append((merged[:, p * cols : (p + 1) * cols] * gain).astype(jnp.bfloat16))
    width = blocks[0].shape[1]
    for i, place in enumerate((h, h ^ 1, h ^ 3 ^ grp, h ^ 2 ^ grp)):
        held[:, pl.ds(pl.multiple_of(place * width, 128), width)] = sum(
            dot(rows[p], blocks[p][i * cols : (i + 1) * cols, :]) for p in range(2)
        )
    keys = 4 * width
    held[:, keys:] = two_terms(squares)
    half, few = held.shape[0] // 2, held.shape[0] // 8
    rounds = matching.shape[0]
    column = lax.broadcasted_iota(jnp.int32, matching.shape, 1) == h
    owner = jnp.sum(jnp.where(column, matching[...], 0), axis=1, keepdims=True)
    lane = lax.broadcasted_iota(jnp.int32, (2 * few, 128), 1)
    for k, out in enumerate(outs):
        start = pl.multiple_of((h ^ k) * few, 8)
        part = jnp.concatenate(
            [held[pl.ds(start, few), :], held[pl.ds(half + start, few), :]], axis=0
        )
        live = sum(
            jnp.where(owner[r : r + 1] == (h ^ k), counts[:, r : r + 1], 0) for r in range(rounds)
        )
        out[:, :keys] = part[:, :keys].astype(out.dtype)
        tail = jnp.where(lane == 32, live.astype(jnp.float32), part[:, keys:])
        out[:, keys:] = tail.astype(out.dtype)


def group_kernel(places, *refs):
    parts, kept, sent, live = refs[:4], refs[4], refs[5], refs[6]
    h = lax.axis_index("hold")
    keys = kept.shape[1] - 128
    total = sum(part[...].astype(jnp.float32) for part in parts)
    for k, part in zip((*places, 0), parts, strict=True):
        live[pl.ds(h ^ k, 1), :] = part[:, keys:].astype(jnp.float32)[:1]
    squares = two_terms(total[:, keys : keys + 1] + total[:, -1:])
    rows = kept.shape[0]
    kept[:, :keys] = total[:rows, :keys]
    kept[:, keys:] = squares[:rows]
    sent[:, :keys] = total[rows:, :keys].astype(jnp.bfloat16)
    sent[:, keys:] = squares[rows:].astype(jnp.bfloat16)


def last_kernel(width, kept, came, matching, live, out):
    h = lax.axis_index("hold")
    _, rounds, block, features = out.shape
    total = kept[...] + came[...].astype(jnp.float32)
    squares = total[:, features : features + 1] + total[:, -1:]
    keys = total[:, :features] * lax.rsqrt(squares / width + EPSILON)
    b_of = lax.broadcasted_iota(jnp.int32, (block, 1), 0).astype(jnp.float32)
    blocks = []
    for i in range(rounds):
        part = keys[i * block : (i + 1) * block]
        blocks.append(jnp.where(b_of < live[i : i + 1, 32:33], part, 0.0))
    for r in range(rounds):
        picked = sum(
            jnp.where(matching[r : r + 1, i : i + 1] == h, blocks[i], 0.0) for i in range(rounds)
        )
        out[0, r] = picked.astype(jnp.bfloat16)


def rows_past_weights(cache, ln_gain, w_fc1, w_fc2, norm_gain, w_key, matching, counts, width):
    n = lax.axis_size("hold")
    rounds, block, depth = cache.shape[1:]
    rows = rounds * block
    chunk = depth // n
    hidden_cols, key_cols = w_fc1.shape[1], w_key.shape[1]
    share = w_key.shape[0] // n
    f32, bf16 = jnp.float32, jnp.bfloat16
    vmem = pltpu.VMEM

    def like(dims, kind=bf16):
        return jax.ShapeDtypeStruct(dims, kind)

    long = 8 << 30
    hbm = pl.BlockSpec(memory_space=pltpu.HBM)
    in_hbm = [
        pltpu.with_memory_space_constraint(x, pltpu.HBM)
        for x in (cache, ln_gain, matching, w_fc1, w_fc2, w_key)
    ]
    cache_other = swap(cache, "tp", 2, 1)
    own, w_fc1_mine, w_fc2_mine, key_0, key_1, key_far = call(
        own_kernel,
        [like((rows, depth), f32), like(w_fc1.shape), like(w_fc2.shape)]
        + [like((share, key_cols))] * 3,
        *in_hbm,
        in_specs=[hbm] * 6,
        scratch=[
            vmem(cache.shape, bf16),
            vmem(ln_gain.shape, f32),
            vmem(matching.shape, jnp.int32),
            pltpu.SemaphoreType.DMA((8,)),
        ],
        flops=long,
    )
    w_fc1_other = swap(w_fc1, "rep", 2, 1)
    gain_other = swap(norm_gain, "rep", 2, 1)
    own, cache_other, w_fc2_sent, w_fc1_other, gain_other = lax.optimization_barrier(
        (own, cache_other, w_fc2_mine, w_fc1_other, gain_other)
    )
    w_fc2_other = swap(w_fc2_sent, "rep", 2, 1)
    pieces = call(
        both_kernel,
        [like((2 * rows, chunk))] * n,
        own,
        cache_other,
        ln_gain,
        matching,
        scratch=[vmem((rows, depth), f32)],
    )

    *pieces, key_1, key_far = lax.optimization_barrier((*pieces, key_1, key_far))
    key_1 = swap(key_1, "hold", n, 1)
    perm = [(n * g + a, n * g + (a ^ 3 ^ g)) for g in range(2) for a in range(n)]
    key_far = lax.ppermute(key_far, ("grp", "hold"), perm)

    order = (3, 2, 1)
    partial = call(
        functools.partial(first_kernel, order),
        [like((4 * rows, hidden_cols))] * n,
        *exchange(pieces, order),
        w_fc1_mine,
        w_fc1_other,
        scratch=[vmem((8 * rows, chunk), f32), vmem((2, 8 * rows, hidden_cols), f32)],
        flops=long,
    )
    *partial, w_fc2_other = lax.optimization_barrier((*partial, w_fc2_other))
    key_near = swap(key_far, "grp", 2, 1)
    parts = exchange(partial, (1, 3, 2))
    hidden = call(gelu_kernel, like(parts[0].shape), *parts, flops=long)
    hidden, key_far = lax.optimization_barrier((hidden, key_far))

    halves = []
    for g in range(2):
        perm = [
            (2 * a + b, 2 * (2 * b + (a >> 1)) + ((a & 1) ^ (a >> 1) ^ b ^ g))
            for a in range(n)
            for b in range(2)
        ]
        halves.append(lax.ppermute(hidden, ("hold", "tp"), perm))
    *halves, key_1 = lax.optimization_barrier((*halves, key_1))
    merged = call(
        second_kernel,
        [like((8 * rows, 2 * share))] * n,
        *halves,
        w_fc2_mine,
        w_fc2_other,
        scratch=[vmem((8 * rows, hidden_cols), bf16)],
        flops=32 * rows * w_fc2.size,
    )
    *merged, key_near = lax.optimization_barrier((*merged, key_near))
    key_mine = jnp.concatenate([key_0, key_1, key_far, key_near])
    key_other = swap(key_mine, "rep", 2, 1)
    wide = n * key_cols + 128
    keys = call(
        key_kernel,
        [like((2 * rows, wide), f32)] + [like((2 * rows, wide))] * (n - 1),
        *exchange(merged, (2, 1, 3)),
        key_mine,
        key_other,
        norm_gain,
        gain_other,
        matching,
        counts.reshape(1, rounds),
        scratch=[vmem((8 * rows, wide), f32)],
        flops=32 * rows * w_key.size,
    )
    order = (3, 1, 2)
    kept, sent, live = call(
        functools.partial(group_kernel, order),
        [like((rows, wide), f32), like((rows, wide)), like((n, 128), f32)],
        *exchange(keys, order),
    )
    return call(
        functools.partial(last_kernel, width),
        like((1, rounds, block, n * key_cols)),
        kept,
        swap(sent, "tp", 2, 1),
        matching,
        live,
    )


def per_device(cache, ln_gain, w_fc1, w_fc2, norm_gain, w_key, matching, counts):
    sizes = lax.axis_size("hold"), lax.axis_size("tp"), lax.axis_size("rep")
    rounds, block, depth = cache.shape[1:]
    group = sizes[1] * sizes[2]
    width = w_key.shape[0] * group
    few = sizes[0] * rounds * group * block <= w_fc1.shape[1]
    fits = sizes == (4, 2, 2) and rounds == 4 and block == 2
    plan = rows_past_weights if few and fits else rows_to_owners
    return plan(cache, ln_gain, w_fc1, w_fc2, norm_gain, w_key, matching, counts, width)


def solution(mesh):
    return jax.shard_map(
        per_device,
        mesh=mesh,
        in_specs=(
            P(("grp", "hold"), None, ("tp", "rep"), None),
            P(),
            P("hold", ("tp", "rep")),
            P("hold", ("tp", "rep")),
            P(("tp", "rep")),
            P(("tp", "rep"), "hold"),
            P("grp", None),
            P(("grp", "hold"), None, ("tp", "rep")),
        ),
        out_specs=P(("grp", "hold"), None, ("tp", "rep"), None),
        check_vma=False,
    )
```

```python
import functools

import jax
import jax.numpy as jnp
from jax import lax
from jax.experimental import pallas as pl
from jax.experimental.pallas import tpu as pltpu
from jax.sharding import PartitionSpec as P

EPSILON = 1e-06
GROUP_AXES = ("tp", "rep")
ALL_AXES = ("hold", "tp", "rep")


def patch_norm(rows, ln_gain):
    width = ln_gain.shape[0]
    patches = rows.astype(jnp.float32).reshape(rows.shape[0], -1, width)
    scale = lax.rsqrt(jnp.mean(patches * patches, axis=2, keepdims=True) + EPSILON)
    return patches * scale * ln_gain


def merger_features(rows, ln_gain, w_fc1, w_fc2, norm_gain, width):
    normed = patch_norm(rows, ln_gain).reshape(rows.shape[0], -1).astype(jnp.bfloat16)
    first_cols = lax.all_gather(w_fc1, "hold", axis=0, tiled=True)
    product = jnp.dot(
        lax.all_gather(normed, GROUP_AXES, axis=0, tiled=True),
        first_cols,
        preferred_element_type=jnp.float32,
    )
    hidden = jax.nn.gelu(product, approximate=False).astype(jnp.bfloat16)
    second_cols = lax.all_gather(w_fc2, "hold", axis=0, tiled=True)
    merged = jnp.dot(
        lax.all_gather(hidden, GROUP_AXES, axis=1, tiled=True),
        second_cols,
        preferred_element_type=jnp.float32,
    )
    squares = lax.psum(jnp.sum(merged * merged, axis=1), GROUP_AXES)
    scale = lax.rsqrt(squares / width + EPSILON)
    return (merged * scale[:, None] * norm_gain).astype(jnp.bfloat16)


def rows_to_owners(cache, ln_gain, w_fc1, w_fc2, norm_gain, w_key, matching, counts, width):
    rounds = cache.shape[1]
    block = cache.shape[2]
    holder_index = lax.axis_index("hold")
    owner_column = lax.dynamic_slice_in_dim(matching, holder_index, 1, 1)[:, 0]
    send_order = jnp.argsort(owner_column)
    source_of = jnp.argmax(matching == holder_index, axis=1)
    sent_counts = jnp.take(counts[0, :, 0], send_order)
    outgoing = jnp.take(cache[0], send_order, axis=0)
    arrived = lax.all_to_all(outgoing, "hold", split_axis=0, concat_axis=0, tiled=True)
    arrived_counts = lax.all_to_all(
        sent_counts.reshape(rounds, 1), "hold", split_axis=0, concat_axis=0, tiled=True
    )
    own_blocks = jnp.take(arrived, source_of, axis=0)
    own_counts = jnp.take(arrived_counts[:, 0], source_of)
    features = merger_features(
        own_blocks.reshape(rounds * block, -1), ln_gain, w_fc1, w_fc2, norm_gain, width
    )
    key_cols = lax.all_gather(w_key, "hold", axis=1, tiled=True)
    keys = lax.psum_scatter(
        jnp.dot(features, key_cols, preferred_element_type=jnp.float32),
        GROUP_AXES,
        scatter_dimension=0,
        tiled=True,
    )
    keys = keys.reshape(rounds, block, -1)
    valid = jnp.arange(block, dtype=jnp.int32)[None, :] < own_counts[:, None]
    keys = jnp.where(valid[:, :, None], keys, jnp.zeros_like(keys))
    return keys.astype(jnp.bfloat16)[None]


def swap(x, axis, n, step):
    return lax.ppermute(x, axis, [(i, i ^ step) for i in range(n)])


def exchange(parts, order):
    n = len(parts)
    return [swap(parts[k], "hold", n, k) for k in order] + [parts[0]]


def call(body, outs, *args, flops=0, scratch=(), **specs):
    moved = sum(x.size * x.dtype.itemsize for x in args)
    return pl.pallas_call(
        body,
        out_shape=outs,
        scratch_shapes=scratch,
        cost_estimate=pl.CostEstimate(flops=flops, bytes_accessed=moved, transcendentals=0),
        compiler_params=pltpu.CompilerParams(vmem_limit_bytes=16 << 20),
        **specs,
    )(*args)


def dot(a, b):
    return jnp.dot(a, b, preferred_element_type=jnp.float32)


def norm_rows(cache, gain, matching, held):
    h = lax.axis_index("hold")
    _, rounds, block, depth = cache.shape
    width = gain.shape[1]
    column = lax.broadcasted_iota(jnp.int32, matching.shape, 1) == h
    owner = jnp.sum(jnp.where(column, matching[...], 0), axis=1, keepdims=True)
    for p in range(depth // width):
        cols = pl.ds(p * width, width)
        normed = []
        for r in range(rounds):
            x = cache[0, r, :, cols].astype(jnp.float32)
            scale = lax.rsqrt(jnp.mean(x * x, axis=1, keepdims=True) + EPSILON)
            normed.append(x * scale * gain)
        for j in range(rounds):
            picked = sum(
                jnp.where(owner[r : r + 1] == j, normed[r], 0.0) for r in range(rounds)
            )
            held[j * block : (j + 1) * block, cols] = picked


def own_kernel(cache, ln_gain, matching, w_fc1, w_fc2, w_key, *refs):
    out, held_1, held_2, *key_rows = refs[:6]
    x_in, gain_in, plan_in, sems = refs[6:]
    h, grp = lax.axis_index("hold"), lax.axis_index("grp")
    pairs = [(cache, x_in), (ln_gain, gain_in), (matching, plan_in), (w_fc1, held_1), (w_fc2, held_2)]
    share = key_rows[0].shape[0]
    for place, end in zip((h, h ^ 1, h ^ 3 ^ grp), key_rows, strict=True):
        pairs.append((w_key.at[pl.ds(pl.multiple_of(place * share, 128), share)], end))
    copies = [pltpu.make_async_copy(a, b, sems.at[i]) for i, (a, b) in enumerate(pairs)]
    for copy in copies:
        copy.start()
    for copy in copies[:3]:
        copy.wait()
    norm_rows(x_in, gain_in[...].reshape(1, -1), plan_in, out)
    for copy in copies[3:]:
        copy.wait()


def both_kernel(own, cache, ln_gain, matching, *refs):
    outs, held = refs[:4], refs[4]
    h = lax.axis_index("hold")
    norm_rows(cache, ln_gain[...].reshape(1, -1), matching, held)
    chunk = outs[0].shape[1]
    for s, out in enumerate(outs):
        cols = pl.ds(pl.multiple_of((h ^ s) * chunk, 128), chunk)
        out[...] = jnp.concatenate([own[:, cols], held[:, cols]], axis=0).astype(jnp.bfloat16)


def first_kernel(places, *refs):
    pieces, weights, outs = refs[:4], refs[4:6], refs[6:10]
    rows = refs[10]
    h, rep = lax.axis_index("hold"), lax.axis_index("rep")
    size = pieces[0].shape[0] // 2
    half = 4 * size
    for k, piece in zip((*places, 0), pieces, strict=True):
        part = piece[...].astype(jnp.float32)
        for b in range(2):
            start = pl.multiple_of(b * half + (h ^ k) * size, 8)
            rows[pl.ds(start, size), :] = part[b * size : (b + 1) * size]
    x = rows[...].astype(jnp.bfloat16)
    mine, other = (dot(x, weight[...]).astype(jnp.bfloat16) for weight in weights)
    for k, out in enumerate(outs):
        part = jnp.where((h ^ k) >> 1 == rep, mine, other)
        out[...] = jnp.where((h ^ k) & 1 == 0, part[:half], part[half:])


ERFC_NEAR = (
    2.326819970068386e-2,
    -1.387039388740657e-1,
    3.687424674597105e-1,
    -5.824733027278666e-1,
    6.210004621745983e-1,
    -4.944515323274145e-1,
    3.404879937665872e-1,
    -2.741127028184656e-1,
    5.638259427386472e-1,
)
ERFC_FAR = (
    -1.047766399936249e1,
    1.297719955372516e1,
    -7.495518717768503e0,
    2.921019019210786e0,
    -1.015265279202700e0,
    4.218463358204948e-1,
    -2.820767439740514e-1,
    5.641895067754075e-1,
)


def erfc(x):
    size = jnp.maximum(jnp.abs(x), 1.0)
    inverse = 1.0 / size
    square = inverse * inverse
    near, far = jnp.zeros_like(x), jnp.zeros_like(x)
    for c in ERFC_NEAR:
        near = near * square + c
    for c in ERFC_FAR:
        far = far * square + c
    tail = jnp.exp(-size * size) * inverse * jnp.where(size < 2.0, near, far)
    return jnp.where(jnp.abs(x) < 1.0, 1.0 - lax.erf(x), jnp.where(x < 0, 2.0 - tail, tail))


def gelu_kernel(*refs):
    x = sum(part[...].astype(jnp.float32) for part in refs[:4])
    hidden = (0.5 * x * erfc(-x * 0.5**0.5)).astype(jnp.bfloat16)
    total = x.shape[0]
    bb = total // 16
    to = lax.broadcasted_iota(jnp.int32, (total, total), 0)
    source = lax.broadcasted_iota(jnp.int32, (total, total), 1)
    owner, holder = to // (4 * bb), (to % (4 * bb)) // bb
    order = jnp.where(source == (holder * 4 + owner) * bb + to % bb, 1.0, 0.0)
    refs[4][...] = dot(order.astype(jnp.bfloat16), hidden).astype(jnp.bfloat16)


def second_kernel(first, second, w_mine, w_other, *refs):
    outs, rows = refs[:4], refs[4]
    h = lax.axis_index("hold")
    half = first.shape[0]
    for g, part in enumerate((first, second)):
        rows[pl.ds(pl.multiple_of((g ^ (h & 1)) * half, 16), half), :] = part[...]
    x = rows[...]
    cols = outs[0].shape[1] // 2
    for p, weight in enumerate((w_mine, w_other)):
        for k, out in enumerate(outs):
            start = pl.multiple_of((h ^ k) * cols, 128)
            part = dot(x, weight[:, pl.ds(start, cols)]).astype(jnp.bfloat16)
            out[:, p * cols : (p + 1) * cols] = part


def two_terms(x):
    high = x.astype(jnp.bfloat16).astype(jnp.float32)
    lane = lax.broadcasted_iota(jnp.int32, (x.shape[0], 128), 1)
    return jnp.where(lane < 64, high, x - high)


def key_kernel(*refs):
    parts, blocks, gains, matching, counts = refs[:4], refs[4:6], refs[6:8], refs[8], refs[9]
    outs, held = refs[10:14], refs[14]
    h, grp = lax.axis_index("hold"), lax.axis_index("grp")
    merged = sum(part[...].astype(jnp.float32) for part in parts)
    squares = jnp.sum(merged * merged, axis=1, keepdims=True)
    cols = merged.shape[1] // 2
    start = pl.multiple_of(h * cols, 128)
    rows = []
    for p in range(2):
        gain = gains[p][pl.ds(start, cols)].reshape(1, cols)
        rows.append((merged[:, p * cols : (p + 1) * cols] * gain).astype(jnp.bfloat16))
    width = blocks[0].shape[1]
    for i, place in enumerate((h, h ^ 1, h ^ 3 ^ grp, h ^ 2 ^ grp)):
        held[:, pl.ds(pl.multiple_of(place * width, 128), width)] = sum(
            dot(rows[p], blocks[p][i * cols : (i + 1) * cols, :]) for p in range(2)
        )
    keys = 4 * width
    held[:, keys:] = two_terms(squares)
    half, few = held.shape[0] // 2, held.shape[0] // 8
    rounds = matching.shape[0]
    column = lax.broadcasted_iota(jnp.int32, matching.shape, 1) == h
    owner = jnp.sum(jnp.where(column, matching[...], 0), axis=1, keepdims=True)
    lane = lax.broadcasted_iota(jnp.int32, (2 * few, 128), 1)
    for k, out in enumerate(outs):
        start = pl.multiple_of((h ^ k) * few, 8)
        part = jnp.concatenate(
            [held[pl.ds(start, few), :], held[pl.ds(half + start, few), :]], axis=0
        )
        live = sum(
            jnp.where(owner[r : r + 1] == (h ^ k), counts[:, r : r + 1], 0) for r in range(rounds)
        )
        out[:, :keys] = part[:, :keys].astype(out.dtype)
        tail = jnp.where(lane == 32, live.astype(jnp.float32), part[:, keys:])
        out[:, keys:] = tail.astype(out.dtype)


def group_kernel(places, *refs):
    parts, kept, sent, live = refs[:4], refs[4], refs[5], refs[6]
    h = lax.axis_index("hold")
    keys = kept.shape[1] - 128
    total = sum(part[...].astype(jnp.float32) for part in parts)
    for k, part in zip((*places, 0), parts, strict=True):
        live[pl.ds(h ^ k, 1), :] = part[:, keys:].astype(jnp.float32)[:1]
    squares = two_terms(total[:, keys : keys + 1] + total[:, -1:])
    rows = kept.shape[0]
    kept[:, :keys] = total[:rows, :keys]
    kept[:, keys:] = squares[:rows]
    sent[:, :keys] = total[rows:, :keys].astype(jnp.bfloat16)
    sent[:, keys:] = squares[rows:].astype(jnp.bfloat16)


def last_kernel(width, kept, came, matching, live, out):
    h = lax.axis_index("hold")
    _, rounds, block, features = out.shape
    total = kept[...] + came[...].astype(jnp.float32)
    squares = total[:, features : features + 1] + total[:, -1:]
    keys = total[:, :features] * lax.rsqrt(squares / width + EPSILON)
    b_of = lax.broadcasted_iota(jnp.int32, (block, 1), 0).astype(jnp.float32)
    blocks = []
    for i in range(rounds):
        part = keys[i * block : (i + 1) * block]
        blocks.append(jnp.where(b_of < live[i : i + 1, 32:33], part, 0.0))
    for r in range(rounds):
        picked = sum(
            jnp.where(matching[r : r + 1, i : i + 1] == h, blocks[i], 0.0) for i in range(rounds)
        )
        out[0, r] = picked.astype(jnp.bfloat16)


def rows_past_weights(cache, ln_gain, w_fc1, w_fc2, norm_gain, w_key, matching, counts, width):
    n = lax.axis_size("hold")
    rounds, block, depth = cache.shape[1:]
    rows = rounds * block
    chunk = depth // n
    hidden_cols, key_cols = w_fc1.shape[1], w_key.shape[1]
    share = w_key.shape[0] // n
    f32, bf16 = jnp.float32, jnp.bfloat16
    vmem = pltpu.VMEM

    def like(dims, kind=bf16):
        return jax.ShapeDtypeStruct(dims, kind)

    long = 8 << 30
    hbm = pl.BlockSpec(memory_space=pltpu.HBM)
    in_hbm = [
        pltpu.with_memory_space_constraint(x, pltpu.HBM)
        for x in (cache, ln_gain, matching, w_fc1, w_fc2, w_key)
    ]
    cache_other = swap(cache, "tp", 2, 1)
    own, w_fc1_mine, w_fc2_mine, key_0, key_1, key_far = call(
        own_kernel,
        [like((rows, depth), f32), like(w_fc1.shape), like(w_fc2.shape)]
        + [like((share, key_cols))] * 3,
        *in_hbm,
        in_specs=[hbm] * 6,
        scratch=[
            vmem(cache.shape, bf16),
            vmem(ln_gain.shape, f32),
            vmem(matching.shape, jnp.int32),
            pltpu.SemaphoreType.DMA((8,)),
        ],
        flops=long,
    )
    w_fc1_other = swap(w_fc1, "rep", 2, 1)
    gain_other = swap(norm_gain, "rep", 2, 1)
    own, cache_other, w_fc2_sent, w_fc1_other, gain_other = lax.optimization_barrier(
        (own, cache_other, w_fc2_mine, w_fc1_other, gain_other)
    )
    w_fc2_other = swap(w_fc2_sent, "rep", 2, 1)
    pieces = call(
        both_kernel,
        [like((2 * rows, chunk))] * n,
        own,
        cache_other,
        ln_gain,
        matching,
        scratch=[vmem((rows, depth), f32)],
    )

    *pieces, key_1, key_far = lax.optimization_barrier((*pieces, key_1, key_far))
    key_1 = swap(key_1, "hold", n, 1)
    perm = [(n * g + a, n * g + (a ^ 3 ^ g)) for g in range(2) for a in range(n)]
    key_far = lax.ppermute(key_far, ("grp", "hold"), perm)

    order = (3, 2, 1)
    partial = call(
        functools.partial(first_kernel, order),
        [like((4 * rows, hidden_cols))] * n,
        *exchange(pieces, order),
        w_fc1_mine,
        w_fc1_other,
        scratch=[vmem((8 * rows, chunk), f32)],
        flops=long,
    )
    *partial, w_fc2_other = lax.optimization_barrier((*partial, w_fc2_other))
    key_near = swap(key_far, "grp", 2, 1)
    parts = exchange(partial, (1, 3, 2))
    hidden = call(gelu_kernel, like(parts[0].shape), *parts, flops=long)
    hidden, key_far = lax.optimization_barrier((hidden, key_far))

    halves = []
    for g in range(2):
        perm = [
            (2 * a + b, 2 * (2 * b + (a >> 1)) + ((a & 1) ^ (a >> 1) ^ b ^ g))
            for a in range(n)
            for b in range(2)
        ]
        halves.append(lax.ppermute(hidden, ("hold", "tp"), perm))
    *halves, key_1 = lax.optimization_barrier((*halves, key_1))
    merged = call(
        second_kernel,
        [like((8 * rows, 2 * share))] * n,
        *halves,
        w_fc2_mine,
        w_fc2_other,
        scratch=[vmem((8 * rows, hidden_cols), bf16)],
        flops=32 * rows * w_fc2.size,
    )
    *merged, key_near = lax.optimization_barrier((*merged, key_near))
    key_mine = jnp.concatenate([key_0, key_1, key_far, key_near])
    key_other = swap(key_mine, "rep", 2, 1)
    wide = n * key_cols + 128
    keys = call(
        key_kernel,
        [like((2 * rows, wide), f32)] + [like((2 * rows, wide))] * (n - 1),
        *exchange(merged, (2, 1, 3)),
        key_mine,
        key_other,
        norm_gain,
        gain_other,
        matching,
        counts.reshape(1, rounds),
        scratch=[vmem((8 * rows, wide), f32)],
        flops=32 * rows * w_key.size,
    )
    order = (3, 1, 2)
    kept, sent, live = call(
        functools.partial(group_kernel, order),
        [like((rows, wide), f32), like((rows, wide)), like((n, 128), f32)],
        *exchange(keys, order),
    )
    return call(
        functools.partial(last_kernel, width),
        like((1, rounds, block, n * key_cols)),
        kept,
        swap(sent, "tp", 2, 1),
        matching,
        live,
    )


def per_device(cache, ln_gain, w_fc1, w_fc2, norm_gain, w_key, matching, counts):
    sizes = lax.axis_size("hold"), lax.axis_size("tp"), lax.axis_size("rep")
    rounds, block, depth = cache.shape[1:]
    group = sizes[1] * sizes[2]
    width = w_key.shape[0] * group
    few = sizes[0] * rounds * group * block <= w_fc1.shape[1]
    fits = sizes == (4, 2, 2) and rounds == 4 and block == 2
    plan = rows_past_weights if few and fits else rows_to_owners
    return plan(cache, ln_gain, w_fc1, w_fc2, norm_gain, w_key, matching, counts, width)


def solution(mesh):
    return jax.shard_map(
        per_device,
        mesh=mesh,
        in_specs=(
            P(("grp", "hold"), None, ("tp", "rep"), None),
            P(),
            P("hold", ("tp", "rep")),
            P("hold", ("tp", "rep")),
            P(("tp", "rep")),
            P(("tp", "rep"), "hold"),
            P("grp", None),
            P(("grp", "hold"), None, ("tp", "rep")),
        ),
        out_specs=P(("grp", "hold"), None, ("tp", "rep"), None),
        check_vma=False,
    )
```
